128 devices in a mesh: dp: 32 (over x, y, core), ctx: 4 (over z).
Axes of the slice: x: 4, y: 4, z: 4, core: 2. Of those that a mesh axis runs over, the one named last changes fastest.
Arguments:
- tokens: bfloat16 [32768, 1024], P(('dp', 'ctx')), may hold values from -6 to 6
- send_rows: int32 [128, 256], P(('dp', 'ctx')), may hold values from 0 to 255, each once within a row
- user_lengths: int32 [32, 3], P('dp'), may hold values from 1 to 512, 1024 in all within a row
- input_weight: bfloat16 [1024, 4096], replicated, may hold values from -0.1875 to 0.1875
- output_weight: bfloat16 [1024, 1024], replicated, may hold values from -0.1875 to 0.1875
- distance_bias: float32 [8, 12], replicated, may hold values from 0.5 to 2.5
- upstream: bfloat16 [32768, 1024], P(('dp', 'ctx')), may hold values from -6 to 6
Outputs:
- layer_output: bfloat16 [32768, 1024], P(('dp', 'ctx'))
- token_gradient: bfloat16 [32768, 1024], P(('dp', 'ctx'))
- input_gradient: float32 [1024, 4096], P(('dp', 'ctx'))
- output_gradient: float32 [1024, 1024], P(('dp', 'ctx'))
- bias_gradient: float32 [8, 12], replicated
The draws below stay inside these ranges and needn't reach their ends.
Inputs may be any that keep to these rules, and one draw needn't show every extreme that they name: Each device's row of send_rows is a permutation of its 256 local rows; entry j names the row that goes to dp index j // 8, into slot j % 8. `user_lengths`: row d holds the history lengths of the 3 users of dp index d in buffer order; they sum to 1024 and the longest is 512.
All inputs are finite; a program needn't handle non-finite values.
Results may differ from the reference program's by a relative error of at most 0.0095.
Values may be sent and summed in bfloat16 or wider, within the bound.
A program may use at most 192 MiB of HBM per device.

```python
import math
import jax
import jax.numpy as jnp
import numpy as np
from jax import lax

D = 1024
H = 8
DH = 128
NB = 12
USERS = 3
R = 256
SLOTS = 8
LEN = 1024
ROWS = 32768
N_DP = 32
N_CTX = 4


def level_of(own_key, shape, cuts, smallest, largest):
    def one(position, blocks):
        steps = jax.random.uniform(jax.random.fold_in(jax.random.fold_in(own_key, 6), position), (blocks,), jnp.float32, smallest / len(cuts), largest / len(cuts))
        return jnp.repeat(jnp.exp(steps), shape[position] // blocks).reshape((-1,) + (1,) * (len(shape) - position - 1))

    factor_of = one(*cuts[0])
    for cut in cuts[1:]:
        factor_of = factor_of * one(*cut)
    return factor_of


def length_profile(number_of, total, most, lean):
    weights = [(1 << 20) // math.isqrt(grade ** lean) + 1 for grade in range(2, number_of + 1)]
    spare, given = total - most - (number_of - 1), [1] * (number_of - 1)
    while spare > 0:
        candidates = [i for i in range(number_of - 1) if given[i] < most]
        whole, left = sum([weights[i] for i in candidates]), spare
        for i in candidates:
            addition = min(most - given[i], max(1, left * weights[i] // whole), spare)
            given[i] = given[i] + addition
            spare = spare - addition
    return np.array([most] + given)


def ragged_sizes(rng, number_of, total, bound, slope):
    if number_of == 2:
        one = jax.random.randint(rng, (), max(1, total - bound), min(bound, total - 1) + 1)
        return jnp.stack([one, total - one])
    tallies = jnp.asarray(length_profile(number_of, total, bound, slope), jnp.int32)
    couples = (number_of - 1) // 2
    donor, receiver = tallies[1:1 + 2 * couples:2], tallies[2:2 + 2 * couples:2]
    margin = jnp.minimum(donor - 1, bound - receiver)
    moved = jax.random.randint(jax.random.fold_in(rng, 1), (couples,), 0, 1 << 20) % (margin + 1)
    tallies = tallies.at[1:1 + 2 * couples:2].set(donor - moved).at[2:2 + 2 * couples:2].set(receiver + moved)
    return tallies[jax.random.permutation(jax.random.fold_in(rng, 2), number_of)]


def bell_draw(stream_key, dims, spread, bound, shards=(), kind=jnp.bfloat16):
    values = spread * jax.random.normal(stream_key, dims, jnp.float32)
    if shards:
        values = values * level_of(stream_key, dims, shards, -0.22, 0.18)
    return jnp.clip(values, -bound, bound).astype(kind)


def setup_inputs(seed: int = 0) -> dict:
    streams_of = jax.random.split(jax.random.key(seed), 8)
    return {
        "tokens": bell_draw(streams_of[0], (ROWS, D), 1.0, 6.0, ((0, 128),)),
        "send_rows": jax.vmap(lambda own: jax.random.permutation(own, R))(jax.random.split(streams_of[1], (N_DP * N_CTX))).reshape((N_DP * N_CTX, R)).astype(jnp.int32),
        "user_lengths": jax.vmap(lambda own: ragged_sizes(own, USERS, LEN, LEN // 2, 2))(jax.random.split(streams_of[2], N_DP)).reshape((N_DP, USERS)).astype(jnp.int32),
        "input_weight": bell_draw(streams_of[3], (D, 4 * H * DH), D ** -0.5, 0.1875),
        "output_weight": bell_draw(streams_of[4], (H * DH, D), (H * DH) ** -0.5, 0.1875),
        "distance_bias": jnp.clip(jnp.exp(jax.random.uniform(streams_of[5], (H, NB), jnp.float32, math.log(0.5), math.log(2.5))), 0.5, 2.5),
        "upstream": bell_draw(streams_of[6], (ROWS, D), 1.0, 6.0, ((0, 128),)),
    }


EPSILON = 1e-05
HIGHEST = lax.Precision.HIGHEST

def layer_norm(values):
    row_mean = lax.optimization_barrier(jnp.mean(values, axis=-1, keepdims=True))
    centered = values - row_mean
    inverse = lax.rsqrt(lax.optimization_barrier(jnp.mean(centered * centered, axis=-1, keepdims=True)) + EPSILON)
    return (centered * inverse, inverse)

def norm_backward(unit_rows, inverse_rows, upstream_rows):
    mean_plain = lax.optimization_barrier(jnp.mean(upstream_rows, axis=-1, keepdims=True))
    mean_cross = lax.optimization_barrier(jnp.mean(upstream_rows * unit_rows, axis=-1, keepdims=True))
    return inverse_rows * (upstream_rows - mean_plain - unit_rows * mean_cross)

def silu_slope(values):
    logistic = jax.nn.sigmoid(values)
    return logistic * (1.0 + values * (1.0 - logistic))

def attention_pattern(query_index, key_index, lengths, bucket_count):
    user_ends = jnp.cumsum(lengths, dtype=jnp.int32)
    query_user = lax.optimization_barrier(jnp.sum((query_index[:, None] >= user_ends[None, :]).astype(jnp.int32), axis=1, dtype=jnp.int32))
    key_user = lax.optimization_barrier(jnp.sum((key_index[:, None] >= user_ends[None, :]).astype(jnp.int32), axis=1, dtype=jnp.int32))
    distance = query_index[:, None] - key_index[None, :]
    visible = jnp.logical_and(query_user[:, None] == key_user[None, :], distance >= 0).astype(jnp.float32)
    bucket = jnp.zeros(distance.shape, jnp.int32)
    for level_step in range(1, bucket_count):
        bucket = bucket + (distance + 1 >= 2 ** level_step).astype(jnp.int32)
    levels = jnp.arange(bucket_count, dtype=jnp.int32)
    onehot = (bucket[None, :, :] == levels[:, None, None]).astype(jnp.float32)
    return (visible, onehot)

def group_pass(group_tokens, lengths, upstream, input_weight, output_weight, distance_bias):
    length_all = group_tokens.shape[0]
    feature_width = H * DH
    score_scale = DH ** (-0.5)
    positions = jnp.arange(length_all, dtype=jnp.int32)
    visible, onehot = attention_pattern(positions, positions, lengths, NB)
    features = group_tokens.astype(jnp.float32)
    unit_in, inverse_in = layer_norm(features)
    normed_in = unit_in.astype(jnp.bfloat16)
    projected = jnp.dot(normed_in, input_weight, preferred_element_type=jnp.float32)
    activated = lax.optimization_barrier(jax.nn.silu(projected).astype(jnp.bfloat16)).astype(jnp.float32)
    gate_float = activated[:, :feature_width]
    value_heads = activated[:, feature_width:2 * feature_width].reshape(length_all, H, DH)
    query_heads = activated[:, 2 * feature_width:3 * feature_width].reshape(length_all, H, DH)
    key_heads = activated[:, 3 * feature_width:].reshape(length_all, H, DH)
    bias_rows = jnp.dot(distance_bias, onehot.reshape(NB, -1), precision=HIGHEST).reshape(H, length_all, length_all)
    scores = jnp.einsum('qhd,khd->hqk', query_heads, key_heads, precision=HIGHEST) * score_scale + bias_rows
    weights = lax.optimization_barrier((jax.nn.silu(scores) * visible[None]).astype(jnp.bfloat16)).astype(jnp.float32)
    attended = jnp.einsum('hqk,khd->qhd', weights, value_heads, precision=HIGHEST).reshape(length_all, feature_width)
    unit_out, inverse_out = layer_norm(attended)
    gated_rows = (unit_out * gate_float).astype(jnp.bfloat16)
    layer_out = (features + jnp.dot(gated_rows, output_weight, preferred_element_type=jnp.float32)).astype(jnp.bfloat16)
    gated_gradient = jnp.dot(upstream, output_weight.T, preferred_element_type=jnp.float32)
    output_part = jnp.dot(gated_rows.T, upstream, preferred_element_type=jnp.float32)
    gate_gradient = gated_gradient * unit_out
    attended_gradient = norm_backward(unit_out, inverse_out, gated_gradient * gate_float)
    attended_heads = lax.optimization_barrier(attended_gradient.astype(jnp.bfloat16)).astype(jnp.float32)
    attended_heads = attended_heads.reshape(length_all, H, DH)
    weight_gradient = jnp.einsum('qhd,khd->hqk', attended_heads, value_heads, precision=HIGHEST)
    score_gradient = weight_gradient * silu_slope(scores) * visible[None]
    bias_part = jnp.dot(score_gradient.reshape(H, -1), onehot.reshape(NB, -1).T, precision=HIGHEST)
    score_rounded = lax.optimization_barrier(score_gradient.astype(jnp.bfloat16)).astype(jnp.float32)
    query_gradient = jnp.einsum('hqk,khd->qhd', score_rounded, key_heads, precision=HIGHEST) * score_scale
    key_gradient = jnp.einsum('hqk,qhd->khd', score_rounded, query_heads, precision=HIGHEST) * score_scale
    value_gradient = jnp.einsum('hqk,qhd->khd', weights, attended_heads, precision=HIGHEST)
    joined = jnp.concatenate([gate_gradient, value_gradient.reshape(length_all, feature_width), query_gradient.reshape(length_all, feature_width), key_gradient.reshape(length_all, feature_width)], axis=1)
    projected_gradient = (joined * silu_slope(projected)).astype(jnp.bfloat16)
    input_part = jnp.dot(normed_in.T, projected_gradient, preferred_element_type=jnp.float32)
    normed_gradient = jnp.dot(projected_gradient, input_weight.T, preferred_element_type=jnp.float32)
    balanced_gradient = (upstream.astype(jnp.float32) + norm_backward(unit_in, inverse_in, normed_gradient)).astype(jnp.bfloat16)
    return (layer_out, balanced_gradient, input_part, output_part, bias_part)

def reference(tokens, send_rows, user_lengths, input_weight, output_weight, distance_bias, upstream):
    blocks = tokens.reshape(N_DP, N_CTX, R, D)
    send_lists = send_rows.reshape(N_DP, N_CTX, R)
    picked = jax.vmap(jax.vmap(lambda block_rows, order_list: jnp.take(block_rows, order_list, axis=0)))(blocks, send_lists)
    picked = picked.reshape(N_DP, N_CTX, N_DP, SLOTS, D)
    balanced = jnp.transpose(picked, (2, 1, 0, 3, 4)).reshape(N_DP, N_CTX * R, D)
    upstream_groups = upstream.reshape(N_DP, N_CTX * R, D)

    def step_group(totals, group_inputs):
        group_tokens, lengths, group_upstream = group_inputs
        results = group_pass(group_tokens, lengths, group_upstream, input_weight, output_weight, distance_bias)
        summed = (totals[0] + results[2], totals[1] + results[3], totals[2] + results[4])
        return (summed, (results[0], results[1]))
    initial = (jnp.zeros((D, 4 * H * DH), jnp.float32), jnp.zeros((H * DH, D), jnp.float32), jnp.zeros((H, NB), jnp.float32))
    totals, (layer_rows, gradient_rows) = lax.scan(step_group, initial, (balanced, user_lengths, upstream_groups))
    spread_back = gradient_rows.reshape(N_DP, N_CTX, N_DP, SLOTS, D)
    spread_back = jnp.transpose(spread_back, (2, 1, 0, 3, 4)).reshape(N_DP, N_CTX, R, D)
    token_gradient = jax.vmap(jax.vmap(lambda block_rows, order_list: jnp.zeros_like(block_rows).at[order_list].set(block_rows)))(spread_back, send_lists)
    layer_output = layer_rows.reshape(N_DP * N_CTX * R, D)
    token_gradient = token_gradient.reshape(N_DP * N_CTX * R, D)
    return (layer_output, token_gradient, totals[0], totals[1], totals[2])
```

```python
import jax
import jax.numpy as jnp
from jax import lax
from jax.sharding import PartitionSpec as P

H = 8
DH = 128
NB = 12
N_CTX = 4
EPSILON = 1e-05


def layer_norm(values):
    row_mean = jnp.mean(values, axis=-1, keepdims=True)
    centered = values - row_mean
    inverse = lax.rsqrt(jnp.mean(centered * centered, axis=-1, keepdims=True) + EPSILON)
    return (centered * inverse, inverse)


def norm_backward(unit_rows, inverse_rows, upstream_rows):
    mean_plain = jnp.mean(upstream_rows, axis=-1, keepdims=True)
    mean_cross = jnp.mean(upstream_rows * unit_rows, axis=-1, keepdims=True)
    return inverse_rows * (upstream_rows - mean_plain - unit_rows * mean_cross)


def silu_slope(values):
    logistic = jax.nn.sigmoid(values)
    return logistic * (1.0 + values * (1.0 - logistic))


def dot(a, b, dims):
    return lax.dot_general(a, b, (dims, ((), ())), preferred_element_type=jnp.float32)


def shards(tokens, send_rows, user_lengths, input_weight, output_weight, distance_bias, upstream):
    rows, width = tokens.shape
    groups = lax.axis_size("dp")
    slots = rows // groups
    length = rows * N_CTX
    cols = width // N_CTX
    scale = DH ** (-0.5)
    ctx = lax.axis_index("ctx")
    send_order = send_rows[0]
    lengths = user_lengths[0]
    ordered = jnp.take(tokens, send_order, axis=0).reshape(groups, slots, width)
    balanced = lax.all_to_all(ordered, "dp", split_axis=0, concat_axis=0, tiled=True).reshape(rows, width)
    features = balanced.astype(jnp.float32)
    unit_in, inverse_in = layer_norm(features)
    normed = lax.all_gather(unit_in.astype(jnp.bfloat16), "ctx", axis=0, tiled=True)
    own_weight = lax.dynamic_slice_in_dim(input_weight.reshape(width, 4, N_CTX, cols), ctx, 1, axis=2)
    own_weight = own_weight.reshape(width, 4 * cols)
    gg = dot(upstream, output_weight, ((1,), (1,))).astype(jnp.bfloat16)
    gg = lax.all_to_all(gg, "ctx", split_axis=1, concat_axis=0, tiled=True).astype(jnp.float32)

    projected = dot(normed, own_weight, ((1,), (0,)))
    activated = jax.nn.silu(projected).astype(jnp.bfloat16)
    gate, value, query, key = (activated[:, i * cols : (i + 1) * cols] for i in range(4))
    gate = gate.astype(jnp.float32)
    ends = jnp.cumsum(lengths)
    pos = jnp.arange(length)
    user = jnp.sum((pos[:, None] >= ends[None, :]).astype(jnp.int32), axis=1)
    dist = pos[:, None] - pos[None, :]
    visible = jnp.logical_and(user[:, None] == user[None, :], dist >= 0).astype(jnp.float32)
    bucket = jnp.zeros(dist.shape, jnp.int32)
    for level in range(1, NB):
        bucket = bucket + (dist + 1 >= 2**level).astype(jnp.int32)
    own_bias = lax.dynamic_slice_in_dim(distance_bias, ctx * 2, 2, axis=0)
    heads = []
    for h in range(2):
        s = slice(h * DH, (h + 1) * DH)
        bias = jnp.zeros(dist.shape, jnp.float32)
        for level in range(NB):
            bias = jnp.where(bucket == level, own_bias[h, level], bias)
        scores = dot(query[:, s], key[:, s], ((1,), (1,))) * scale + bias
        weights = (jax.nn.silu(scores) * visible).astype(jnp.bfloat16)
        att = dot(weights, value[:, s], ((1,), (0,)))
        heads.append((s, scores, weights, att))
    attended = jnp.concatenate([h[3] for h in heads], axis=1)
    g = gg * gate
    m = jnp.mean(attended, axis=1)
    cent = attended - m[:, None]
    stats = jnp.stack([m, jnp.sum(cent * cent, axis=1), jnp.sum(g, axis=1), jnp.sum(g * cent, axis=1)])
    alls = lax.all_gather(stats, "ctx", axis=0)
    mean = jnp.mean(alls[:, 0], axis=0)
    shift = alls[:, 0] - mean[None]
    var = (jnp.sum(alls[:, 1], axis=0) + cols * jnp.sum(shift * shift, axis=0)) / width
    inv = lax.rsqrt(var + EPSILON)
    g_mean = jnp.sum(alls[:, 2], axis=0) / width
    g_cross = inv * jnp.sum(alls[:, 3] + shift * alls[:, 2], axis=0) / width
    unit_out = (attended - mean[:, None]) * inv[:, None]
    gated = (unit_out * gate).astype(jnp.bfloat16)
    gated_own = lax.all_to_all(gated, "ctx", split_axis=0, concat_axis=1, tiled=True)
    layer_output = (features + dot(gated_own, output_weight, ((1,), (0,)))).astype(jnp.bfloat16)
    output_local = dot(gated_own, upstream, ((0,), (0,)))
    gate_gradient = gg * unit_out
    att_grad = (inv[:, None] * (g - g_mean[:, None] - unit_out * g_cross[:, None])).astype(jnp.bfloat16)
    dq, dk, dv, db = [], [], [], []
    for s, scores, weights, _ in heads:
        dw = dot(att_grad[:, s], value[:, s], ((1,), (1,)))
        ds = dw * silu_slope(scores) * visible
        db.append(jnp.stack([jnp.sum(jnp.where(bucket == level, ds, 0.0)) for level in range(NB)]))
        dsr = ds.astype(jnp.bfloat16)
        dq.append(dot(dsr, key[:, s], ((1,), (0,))) * scale)
        dk.append(dot(dsr, query[:, s], ((0,), (0,))) * scale)
        dv.append(dot(weights, att_grad[:, s], ((0,), (0,))))
    joined = jnp.concatenate([gate_gradient] + dv + dq + dk, axis=1)
    pg = (joined * silu_slope(projected)).astype(jnp.bfloat16)
    gin = dot(normed, pg, ((0,), (0,))).astype(jnp.bfloat16)
    ng = dot(pg, own_weight, ((1,), (1,))).astype(jnp.bfloat16)
    ng = lax.all_to_all(ng.reshape(N_CTX, rows, width), "ctx", split_axis=0, concat_axis=0, tiled=True)
    ng = jnp.sum(ng.astype(jnp.float32), axis=0)
    balanced_gradient = (upstream.astype(jnp.float32) + norm_backward(unit_in, inverse_in, ng)).astype(jnp.bfloat16)
    returned = lax.all_to_all(
        balanced_gradient.reshape(groups, slots, width), "dp", split_axis=0, concat_axis=0, tiled=True
    )
    token_gradient = jnp.zeros_like(tokens).at[send_order].set(returned.reshape(rows, width))
    per = width // groups
    gin = lax.all_to_all(gin.reshape(groups, per, width), "dp", split_axis=0, concat_axis=0, tiled=True)
    gin = jnp.sum(gin.astype(jnp.float32), axis=0)
    gin = lax.all_to_all(gin.reshape(N_CTX, per // N_CTX, width), "ctx", split_axis=0, concat_axis=0, tiled=True)
    gin = gin.reshape(N_CTX, per // N_CTX, 4, cols).transpose(1, 2, 0, 3).reshape(per // N_CTX, 4 * width)
    gout = output_local.astype(jnp.bfloat16)
    gout = lax.all_to_all(gout.reshape(groups, per, width), "dp", split_axis=0, concat_axis=0, tiled=True)
    gout = jnp.sum(gout.astype(jnp.float32), axis=0)
    gout = lax.psum_scatter(gout, "ctx", scatter_dimension=0, tiled=True)
    own_db = lax.dynamic_update_slice_in_dim(jnp.zeros((H, NB), jnp.float32), jnp.stack(db), ctx * 2, axis=0)
    own_db = jnp.pad(own_db, ((0, 0), (0, 128 - NB)))
    by_ctx = jnp.sum(lax.all_gather(own_db, "ctx", axis=0), axis=0)
    bias_gradient = jnp.sum(lax.all_gather(by_ctx, "dp", axis=0), axis=0)[:, :NB]
    return (layer_output, token_gradient, gin, gout, bias_gradient)


def solution(mesh):
    block = P(("dp", "ctx"), None)
    in_specs = (block, block, P("dp", None), P(), P(), P(), block)
    out_specs = (block, block, block, block, P())
    return jax.shard_map(shards, mesh=mesh, in_specs=in_specs, out_specs=out_specs, check_vma=False)
```

```python
import jax
import jax.numpy as jnp
from jax import lax
from jax.experimental import pallas as pl
from jax.experimental.pallas import tpu as pltpu
from jax.sharding import PartitionSpec as P

H = 8
DH = 128
NB = 12
N_CTX = 4
R = 256
D = 1024
LEN = 1024
COLS = 256
HEADS = 2
EPSILON = 1e-05
SCALE = DH ** (-0.5)
F32 = jnp.float32
BF16 = jnp.bfloat16
MESH = pl.DeviceIdType.MESH
NN = ((1,), (0,))
NT = ((1,), (1,))
TN = ((0,), (0,))


def dot(left, right, dims):
    return lax.dot_general(left, right, (dims, ((), ())), preferred_element_type=F32)


def at(start, size):
    return pl.ds(pl.multiple_of(start, size), size)


def logistic(values):
    return 0.5 * jnp.tanh(0.5 * values) + 0.5


def copy_to(src, dst, send_sem, recv_sem, dp, ctx):
    return pltpu.make_async_remote_copy(
        src_ref=src, dst_ref=dst, send_sem=send_sem, recv_sem=recv_sem, device_id=(dp, ctx), device_id_type=MESH
    )


def split_halves(rows):
    count = rows.shape[0] // 8
    left = rows[:, :512].reshape(count, 1, 8, 512)
    right = rows[:, 512:].reshape(count, 1, 8, 512)
    return jnp.concatenate((left, right), axis=1).reshape(count * 16, 512)


def join_halves(pairs):
    count = pairs.shape[0] // 16
    parts = pairs.reshape(count, 2, 8, 512)
    return jnp.concatenate((parts[:, 0].reshape(count * 8, 512), parts[:, 1].reshape(count * 8, 512)), axis=1)


def kernel(
    tokens, send_rows, lengths, weight_in, weight_out, bias_table, upstream,
    layer_output, token_gradient, input_gradient, output_gradient, bias_gradient,
    w_in, w_out, pick, message, balanced, unit, inverse_in, normed, gg_send, gg_all, slope, act, bias_tile,
    w_tile, s_tile, attended, stats_send, stats_all, rows_stat, gated, gated_all, att_grad, dq, dk, dv, bias_sum, pg,
    ng_far, ng_far_in, ng_near, ng_near_in, ng_own, back, back_in,
    g_core, g_core_in, g_own, g_chip, g_chip_in, g_row, g_row_in,
    b_core, b_core_in, b_chip_in, b_row, b_row_in,
    w_sem, a_send, a_recv, gg_ssem, gg_rsem, z_send, z_recv, f_send, f_recv, st_send, st_recv, gt_send, gt_recv,
    nf_send, nf_recv, nn_send, nn_recv, r_send, r_recv, gc_send, gc_recv, gk_send, gk_recv, gr_send, gr_recv,
    bc_send, bc_recv, bk_send, bk_recv, br_send, br_recv,
):
    me = lax.axis_index("dp")
    ctx = lax.axis_index("ctx")
    plane, inner = me // 8, me % 8
    chip, core = me // 2, me % 2
    partner = chip * 2 + (1 - core)
    right, left, far = (ctx + 1) % 4, (ctx + 3) % 4, (ctx + 2) % 4

    out_copy = pltpu.make_async_copy(weight_out, w_out, w_sem.at[4])
    out_copy.start()
    in_copies = []
    for part in range(4):
        columns = pl.ds(pl.multiple_of(part * D + ctx * COLS, COLS), COLS)
        in_copies.append(pltpu.make_async_copy(weight_in.at[:, columns], w_in.at[part], w_sem.at[part]))
        in_copies[-1].start()

    barrier = pltpu.get_barrier_semaphore()

    @pl.loop(1, 32)
    def _(step):
        pl.semaphore_signal(barrier, inc=1, device_id=((me + step) % 32, ctx), device_id_type=MESH)

    for step in range(1, 4):
        pl.semaphore_signal(barrier, inc=1, device_id=(me, (ctx + step) % 4), device_id_type=MESH)

    rows_of = lax.broadcasted_iota(jnp.int32, (R, R), 0)
    pick[...] = jnp.where(rows_of == send_rows[...], 1.0, 0.0).astype(BF16)
    message[...] = split_halves(dot(pick[...], tokens[...], TN)).astype(BF16)

    pl.semaphore_wait(barrier, 34)

    def token_copy(dst):
        return copy_to(
            message.at[at(dst * 16, 16), :], balanced.at[at(me * 16, 16), :], a_send.at[dst], a_recv.at[me], dst, ctx
        )

    def token_arrival(src):
        return copy_to(
            message.at[at(src * 16, 16), :], balanced.at[at(src * 16, 16), :], a_send.at[src], a_recv.at[src], src, ctx
        )

    @pl.loop(1, 32)
    def _(step):
        p, q = step // 8, step % 8
        token_copy((plane + p) % 4 * 8 + (inner + q) % 8).start()

    balanced[at(me * 16, 16), :] = message[at(me * 16, 16), :]

    out_copy.wait()

    def gg_copy(block):
        return copy_to(
            gg_send.at[block], gg_all.at[ctx], gg_ssem.at[block], gg_rsem.at[ctx], me, block
        )

    for step in (2, 1, 3, 0):
        block = (ctx + step) % 4
        result = dot(upstream[...], w_out[at(block * COLS, COLS), :], NT).astype(BF16)
        if step == 0:
            gg_all[ctx] = result
        else:
            gg_send[block] = result
            gg_copy(block).start()

    def near_copy(p, side):
        rows = at(ctx * R + (plane + 4 - p) % 4 * 64, 64)
        return copy_to(
            normed.at[rows, :], normed.at[rows, :], z_send.at[side, p], z_recv.at[side, p], me, right if side == 0 else left
        )

    def near_arrival(p, side):
        rows = at((left if side == 0 else right) * R + (plane + 4 - p) % 4 * 64, 64)
        return copy_to(
            normed.at[rows, :], normed.at[rows, :], z_send.at[side, p], z_recv.at[side, p], me, right if side == 0 else left
        )

    def far_copy(p, side):
        rows = at((left if side == 0 else right) * R + (plane + 4 - p) % 4 * 64, 64)
        return copy_to(
            normed.at[rows, :], normed.at[rows, :], f_send.at[p], f_recv.at[p], me, right if side == 0 else left
        )

    def far_arrival(p, side):
        rows = at(far * R + (plane + 4 - p) % 4 * 64, 64)
        return copy_to(
            normed.at[rows, :], normed.at[rows, :], f_send.at[p], f_recv.at[p], me, right if side == 0 else left
        )

    for p in range(4):
        source = (plane + 4 - p) % 4

        @pl.loop(1 if p == 0 else 0, 8)
        def _(q):
            token_arrival(source * 8 + (inner + 8 - q) % 8).wait_recv()

        rows = join_halves(balanced[at(source * 128, 128), :].astype(F32))
        mean = jnp.mean(rows, axis=1, keepdims=True)
        centered = rows - mean
        inverse = lax.rsqrt(jnp.mean(centered * centered, axis=1, keepdims=True) + EPSILON)
        values = centered * inverse
        unit[at(source * 64, 64), :] = values
        inverse_in[at(source * 64, 64), :] = jnp.broadcast_to(inverse, (64, 128))
        normed[at(ctx * R + source * 64, 64), :] = values.astype(BF16)
        near_copy(p, 0).start()
        near_copy(p, 1).start()

    for part in range(4):
        in_copies[part].wait()

    def project(block):
        @pl.loop(0, 4)
        def _(part):
            values = dot(normed[at(block * R, R), :], w_in[part], NN)
            gate = logistic(values)
            active = values * gate
            act[part, at(block * R, R), :] = active.astype(BF16)
            slope[part, at(block * R, R), :] = gate + active * (1.0 - gate)

    for p in range(2):
        near_arrival(p, 0).wait_recv()
        far_copy(p, 0).start()

    for hh in range(HEADS):
        for r in range(3):
            reach = (
                lax.broadcasted_iota(jnp.int32, (R, R), 0) - lax.broadcasted_iota(jnp.int32, (R, R), 1) + (r * R + 1)
            )
            low, high = ((0, 8), (1, 9), (8, 9))[r]
            tile = jnp.full((R, R), bias_table[ctx * HEADS + hh, low], F32)
            for level in range(low + 1, high + 1):
                tile = jnp.where(reach >= 2**level, bias_table[ctx * HEADS + hh, level], tile)
            bias_tile[hh * 3 + r] = tile

    project(ctx)
    for p in range(2, 4):
        near_arrival(p, 1).wait_recv()
        far_copy(p, 1).start()
    near_arrival(2, 0).wait_recv()
    near_arrival(3, 0).wait_recv()
    project(left)
    near_arrival(0, 1).wait_recv()
    near_arrival(1, 1).wait_recv()
    project(right)
    far_arrival(0, 0).wait_recv()
    far_arrival(1, 0).wait_recv()
    far_arrival(2, 1).wait_recv()
    far_arrival(3, 1).wait_recv()
    project(far)

    end_0 = lengths[0, 0]
    end_1 = end_0 + lengths[0, 1]
    bases = (0, 4, 7)

    def seen(block, r):
        q_pos = lax.broadcasted_iota(jnp.int32, (R, R), 0) + block * R
        k_pos = lax.broadcasted_iota(jnp.int32, (R, R), 1) + (block - r) * R
        q_user = jnp.where(q_pos >= end_0, 1, 0) + jnp.where(q_pos >= end_1, 1, 0)
        k_user = jnp.where(k_pos >= end_0, 1, 0) + jnp.where(k_pos >= end_1, 1, 0)
        same = q_user == k_user
        if r == 0:
            same = jnp.logical_and(same, q_pos >= k_pos)
        return same

    for r in range(3):
        @pl.loop(r, 4)
        def _(block):
            visible = seen(block, r)
            for hh in range(HEADS):
                cols = slice(hh * DH, hh * DH + DH)
                query = act[2, at(block * R, R), cols]
                keys = act[3, at((block - r) * R, R), cols]
                values = act[1, at((block - r) * R, R), cols]
                scores = dot(query, keys, NT) * SCALE + bias_tile[hh * 3 + r]
                gate = logistic(scores)
                active = scores * gate
                weights = jnp.where(visible, active, 0.0).astype(BF16)
                s_tile[hh, bases[r] + block - r] = jnp.where(visible, gate + active * (1.0 - gate), 0.0)
                w_tile[hh, bases[r] + block - r] = weights
                term = dot(weights, values, NN)
                if r == 0:
                    attended[at(block * R, R), cols] = term
                else:
                    attended[at(block * R, R), cols] += term

    for step in range(1, 4):
        block = (ctx + step) % 4
        copy_to(gg_send.at[block], gg_all.at[block], gg_ssem.at[block], gg_rsem.at[block], me, block).wait_recv()

    lane = lax.broadcasted_iota(jnp.int32, (R, 128), 1)

    @pl.loop(0, 4)
    def _(block):
        rows = attended[at(block * R, R), :]
        mean = jnp.mean(rows, axis=1, keepdims=True)
        centered = rows - mean
        flow = gg_all[block].astype(F32) * act[0, at(block * R, R), :].astype(F32)
        packed = jnp.where(lane == 0, mean, 0.0)
        packed = jnp.where(lane == 1, jnp.sum(centered * centered, axis=1, keepdims=True), packed)
        packed = jnp.where(lane == 2, jnp.sum(flow, axis=1, keepdims=True), packed)
        packed = jnp.where(lane == 3, jnp.sum(flow * centered, axis=1, keepdims=True), packed)
        stats_send[block] = packed.T[:8, :]

    def stats_copy(block):
        return copy_to(stats_send, stats_all.at[ctx], st_send.at[block], st_recv.at[ctx], me, block)

    for step in range(1, 4):
        stats_copy((ctx + step) % 4).start()
    stats_all[ctx] = stats_send[...]
    for step in range(1, 4):
        block = (ctx + step) % 4
        copy_to(stats_send, stats_all.at[block], st_send.at[block], st_recv.at[block], me, block).wait_recv()

    for block in range(4):
        parts = [stats_all[c, block] for c in range(4)]
        means = [x[0:1] for x in parts]
        mean = (means[0] + means[1] + means[2] + means[3]) * 0.25
        square = sum(parts[c][1:2] + COLS * (means[c] - mean) * (means[c] - mean) for c in range(4))
        flow = sum(parts[c][2:3] for c in range(4))
        cross = sum(parts[c][3:4] + (means[c] - mean) * parts[c][2:3] for c in range(4))
        inverse = lax.rsqrt(square * (1.0 / D) + EPSILON)
        table = jnp.concatenate(
            (mean, inverse, flow * (1.0 / D), cross * inverse * (1.0 / D), jnp.zeros((124, R), F32)), axis=0
        )
        rows_stat[pl.ds(block * R, R), :] = table.T

    def gated_copy(block):
        return copy_to(gated.at[block], gated_all.at[ctx], gt_send.at[block], gt_recv.at[ctx], me, block)

    @pl.loop(0, 4)
    def _(block):
        rows = at(block * R, R)
        table = rows_stat[rows, :]
        inverse = table[:, 1:2]
        out_unit = (attended[rows, :] - table[:, 0:1]) * inverse
        gate = act[0, rows, :].astype(F32)
        flow = gg_all[block].astype(F32)
        gated[block] = (out_unit * gate).astype(BF16)
        pg[0, rows, :] = (flow * out_unit * slope[0, rows, :]).astype(BF16)
        att_grad[rows, :] = (inverse * (flow * gate - table[:, 2:3] - out_unit * table[:, 3:4])).astype(BF16)

    for step in range(1, 4):
        gated_copy((ctx + step) % 4).start()
    gated_all[ctx] = gated[ctx]

    def core_copy(which, piece):
        return copy_to(
            g_core.at[which, piece], g_core_in.at[which, piece], gc_send.at[which, piece], gc_recv.at[which, piece],
            partner, ctx,
        )

    def chip_copy(which, other):
        return copy_to(
            g_chip.at[which, other], g_chip_in.at[which, chip], gk_send.at[which, other], gk_recv.at[which, chip],
            other * 2 + core, ctx,
        )

    def chip_arrival(which, other):
        return copy_to(
            g_chip.at[which, other], g_chip_in.at[which, other], gk_send.at[which, other], gk_recv.at[which, other],
            other * 2 + core, ctx,
        )

    def row_copy(which, block):
        return copy_to(
            g_row.at[which, at(block * 8, 8), :], g_row_in.at[which, ctx], gr_send.at[which, block],
            gr_recv.at[which, ctx], me, block,
        )

    def row_arrival(which, block):
        return copy_to(
            g_row.at[which, at(block * 8, 8), :], g_row_in.at[which, block], gr_send.at[which, block],
            gr_recv.at[which, block], me, block,
        )

    def keep_tile(which, piece, column, tile):
        halves = tile.reshape(4, 2, 32, COLS)
        first, second = halves[:, 0].reshape(128, COLS), halves[:, 1].reshape(128, COLS)
        cols = at(column * COLS, COLS)
        g_own[which, piece, :, cols] = jnp.where(core == 0, first, second).astype(BF16)
        g_core[which, piece, :, cols] = jnp.where(core == 0, second, first).astype(BF16)

    def sum_cores(which):
        for piece in range(4):
            core_copy(which, piece).wait_recv()
            both = g_own[which, piece].astype(F32) + g_core_in[which, piece].astype(F32)
            g_chip[which, pl.ds(piece * 4, 4)] = both.astype(BF16).reshape(4, 32, D)

        @pl.loop(1, 16)
        def _(step):
            chip_copy(which, (chip + step) % 16).start()

        g_chip_in[which, chip] = g_chip[which, chip]

    def sum_chips(which):
        @pl.loop(1, 16)
        def _(step):
            chip_arrival(which, (chip + step) % 16).wait_recv()

        for column in range(4):
            cols = slice(column * COLS, column * COLS + COLS)
            total = g_chip_in[which, 0, :, cols].astype(F32)
            for other in range(1, 16):
                total = total + g_chip_in[which, other, :, cols].astype(F32)
            g_row[which, :, cols] = total
        for step in range(1, 4):
            row_copy(which, (ctx + step) % 4).start()
        g_row_in[which, ctx] = g_row[which, at(ctx * 8, 8), :]

    def attention_back(r):
        @pl.loop(r, 4)
        def _(block):
            q_rows = at(block * R, R)
            k_rows = at((block - r) * R, R)
            for hh in range(HEADS):
                cols = slice(hh * DH, hh * DH + DH)
                incoming = att_grad[q_rows, cols]
                change = dot(incoming, act[1, k_rows, cols], NT) * s_tile[hh, bases[r] + block - r]
                if r == 0:
                    first = jnp.where(block == 0, 0.0, 1.0)
                    bias_sum[hh * 3 + r] = bias_sum[hh * 3 + r] * first + change
                else:
                    bias_sum[hh * 3 + r] += change
                rounded = change.astype(BF16)
                q_term = dot(rounded, act[3, k_rows, cols], NN)
                k_term = dot(rounded, act[2, q_rows, cols], TN)
                v_term = dot(w_tile[hh, bases[r] + block - r], incoming, TN)
                if r == 0:
                    dq[q_rows, cols] = q_term
                    dk[k_rows, cols] = k_term
                    dv[k_rows, cols] = v_term
                else:
                    dq[q_rows, cols] += q_term
                    dk[k_rows, cols] += k_term
                    dv[k_rows, cols] += v_term

    bias_sum[...] = jnp.zeros((6, R, R), F32)
    attention_back(0)

    for step in range(1, 4):
        block = (ctx + step) % 4
        copy_to(gated.at[block], gated_all.at[block], gt_send.at[block], gt_recv.at[block], me, block).wait_recv()

    for piece in range(4):
        left_rows = gated_all[piece].T

        @pl.loop(0, 4)
        def _(column):
            keep_tile(1, piece, column, dot(left_rows, upstream[:, at(column * COLS, COLS)], NN))

        core_copy(1, piece).start()

    attention_back(1)
    sum_cores(1)
    attention_back(2)

    @pl.loop(0, 4)
    def _(block):
        rows = at(block * R, R)
        pg[1, rows, :] = (dv[rows, :] * slope[1, rows, :]).astype(BF16)
        pg[2, rows, :] = (dq[rows, :] * SCALE * slope[2, rows, :]).astype(BF16)
        pg[3, rows, :] = (dk[rows, :] * SCALE * slope[3, rows, :]).astype(BF16)

    def block_terms(block, half):
        rows = at(block * R, R)
        total = dot(pg[0, rows, :], w_in[0, half * 512 : half * 512 + 512, :], NT)
        for part in range(1, 4):
            total = total + dot(pg[part, rows, :], w_in[part, half * 512 : half * 512 + 512, :], NT)
        return total

    def far_part(side):
        return copy_to(
            ng_far.at[side], ng_far_in.at[side], nf_send.at[side], nf_recv.at[side], me, right if side == 0 else left
        )

    def near_part(side, half):
        return copy_to(
            ng_near.at[side, half], ng_near_in.at[side, half], nn_send.at[side, half], nn_recv.at[side, half], me,
            right if side == 0 else left,
        )

    for side in range(2):
        ng_far[side] = block_terms(far, side).astype(BF16)
        far_part(side).start()
    for side in range(2):
        ng_near[side, 1 - side] = block_terms(right if side == 0 else left, 1 - side).astype(BF16)
        near_part(side, 1 - side).start()
    for side in range(2):
        terms = block_terms(right if side == 0 else left, side)
        far_part(side).wait_recv()
        ng_near[side, side] = (terms + ng_far_in[side].astype(F32)).astype(BF16)
        near_part(side, side).start()
    for half in range(2):
        ng_own[:, half * 512 : half * 512 + 512] = block_terms(ctx, half)

    for piece in range(4):
        left_rows = normed[:, piece * R : piece * R + R].T

        @pl.loop(0, 4)
        def _(part):
            keep_tile(0, piece, part, dot(left_rows, pg[part], NN))

        core_copy(0, piece).start()
    sum_cores(0)

    for half in range(2):
        cols = slice(half * 512, half * 512 + 512)
        total = dot(gated_all[0], w_out[0:COLS, cols], NN)
        for c in range(1, 4):
            total = total + dot(gated_all[c], w_out[c * COLS : c * COLS + COLS, cols], NN)
        pairs = balanced[...].astype(F32).reshape(32, 2, 8, 512)
        layer_output[:, cols] = (pairs[:, half].reshape(R, 512) + total).astype(BF16)

    sums = jnp.zeros((8, 128), F32)
    tile_row = lax.broadcasted_iota(jnp.int32, (8, 128), 0)
    tile_lane = lax.broadcasted_iota(jnp.int32, (8, 128), 1)
    for hh in range(HEADS):
        for r in range(3):
            reach = (
                lax.broadcasted_iota(jnp.int32, (R, R), 0) - lax.broadcasted_iota(jnp.int32, (R, R), 1) + (r * R + 1)
            )
            low, high = ((0, 8), (1, 9), (8, 9))[r]
            tile = bias_sum[hh * 3 + r]
            for level in range(low, high + 1):
                part = tile
                if level > low:
                    part = jnp.where(reach >= 2**level, part, 0.0)
                if level < high:
                    part = jnp.where(reach < 2 ** (level + 1), part, 0.0)
                total = jnp.sum(jnp.sum(part, axis=0, keepdims=True), axis=1, keepdims=True)
                place = jnp.logical_and(tile_row == ctx * HEADS + hh, tile_lane == level)
                sums = sums + jnp.where(place, total, 0.0)
    b_core[...] = sums
    bias_core = copy_to(b_core, b_core_in, bc_send, bc_recv, partner, ctx)
    bias_core.start()

    for side in range(2):
        for half in range(2):
            near_part(side, half).wait_recv()

    def back_copy(dst):
        return copy_to(
            back.at[at(dst * 16, 16), :], back_in.at[at(me * 16, 16), :], r_send.at[dst], r_recv.at[me], dst, ctx
        )

    def back_arrival(src):
        return copy_to(
            back.at[at(src * 16, 16), :], back_in.at[at(src * 16, 16), :], r_send.at[src], r_recv.at[src], src, ctx
        )

    for p in range(4):
        target = (plane + p) % 4
        rows = at(target * 64, 64)
        total = []
        for half in range(2):
            total.append(
                ng_own[rows, half * 512 : half * 512 + 512]
                + ng_near_in[0, half, rows, :].astype(F32)
                + ng_near_in[1, half, rows, :].astype(F32)
            )
        total = jnp.concatenate(total, axis=1)
        values = unit[rows, :]
        plain = jnp.mean(total, axis=1, keepdims=True)
        cross = jnp.mean(total * values, axis=1, keepdims=True)
        change = inverse_in[rows, 0:1] * (total - plain - values * cross)
        result = upstream[rows, :].astype(F32) + change
        back[at(target * 128, 128), :] = split_halves(result).astype(BF16)

        @pl.loop(1 if p == 0 else 0, 8)
        def _(q):
            back_copy(target * 8 + (inner + q) % 8).start()

    back_in[at(me * 16, 16), :] = back[at(me * 16, 16), :]

    bias_core.wait_recv()
    b_chip_in[chip] = b_core[...] + b_core_in[...]

    def bias_chip(other):
        return copy_to(
            b_chip_in.at[chip], b_chip_in.at[chip], bk_send.at[other], bk_recv.at[chip], other * 2 + core, ctx
        )

    @pl.loop(1, 16)
    def _(step):
        bias_chip((chip + step) % 16).start()

    sum_chips(1)
    sum_chips(0)

    @pl.loop(1, 16)
    def _(step):
        other = (chip + step) % 16
        copy_to(
            b_chip_in.at[other], b_chip_in.at[other], bk_send.at[other], bk_recv.at[other], other * 2 + core, ctx
        ).wait_recv()

    total = b_chip_in[0]
    for other in range(1, 16):
        total = total + b_chip_in[other]
    b_row[...] = total
    b_row_in[ctx] = total
    for step in range(1, 4):
        block = (ctx + step) % 4
        copy_to(b_row, b_row_in.at[ctx], br_send.at[block], br_recv.at[ctx], me, block).start()

    @pl.loop(1, 32)
    def _(step):
        back_arrival((me + step) % 32).wait_recv()

    returned = join_halves(back_in[...].astype(F32)).astype(BF16)
    token_gradient[...] = dot(pick[...], returned, NN).astype(BF16)

    for step in range(1, 4):
        block = (ctx + step) % 4
        row_arrival(0, block).wait_recv()
        row_arrival(1, block).wait_recv()
        copy_to(b_row, b_row_in.at[block], br_send.at[block], br_recv.at[block], me, block).wait_recv()
    for c in range(4):
        for part in range(4):
            input_gradient[:, part * D + c * COLS : part * D + c * COLS + COLS] = g_row_in[
                0, c, :, part * COLS : part * COLS + COLS
            ]
    output_gradient[...] = g_row_in[1, 0] + g_row_in[1, 1] + g_row_in[1, 2] + g_row_in[1, 3]
    bias_gradient[...] = b_row_in[0] + b_row_in[1] + b_row_in[2] + b_row_in[3]

    @pl.loop(1, 32)
    def _(step):
        other = (me + step) % 32
        token_copy(other).wait_send()
        back_copy(other).wait_send()

    for p in range(4):
        near_copy(p, 0).wait_send()
        near_copy(p, 1).wait_send()
        far_copy(p, 0 if p < 2 else 1).wait_send()
    for step in range(1, 4):
        block = (ctx + step) % 4
        gg_copy(block).wait_send()
        stats_copy(block).wait_send()
        gated_copy(block).wait_send()
        row_copy(0, block).wait_send()
        row_copy(1, block).wait_send()
        copy_to(b_row, b_row_in.at[ctx], br_send.at[block], br_recv.at[ctx], me, block).wait_send()
    for side in range(2):
        far_part(side).wait_send()
        near_part(side, 0).wait_send()
        near_part(side, 1).wait_send()
    for which in range(2):
        for piece in range(4):
            core_copy(which, piece).wait_send()

        @pl.loop(1, 16)
        def _(step):
            chip_copy(which, (chip + step) % 16).wait_send()

    bias_core.wait_send()

    @pl.loop(1, 16)
    def _(step):
        bias_chip((chip + step) % 16).wait_send()


def shards(tokens, send_rows, user_lengths, input_weight, output_weight, distance_bias, upstream):
    vmem = pl.BlockSpec(memory_space=pltpu.VMEM)
    smem = pl.BlockSpec(memory_space=pltpu.SMEM)
    hbm = pl.BlockSpec(memory_space=pl.ANY)
    dma = pltpu.SemaphoreType.DMA
    V = pltpu.VMEM
    scratch = [
        V((4, D, COLS), BF16), V((D, D), BF16), V((R, R), BF16), V((512, 512), BF16), V((512, 512), BF16),
        V((R, D), F32), V((R, 128), F32), V((LEN, D), BF16), V((4, R, COLS), BF16), V((4, R, COLS), BF16),
        V((4, LEN, COLS), F32), V((4, LEN, COLS), BF16), V((6, R, R), F32),
        V((HEADS, 9, R, R), BF16), V((HEADS, 9, R, R), F32), V((LEN, COLS), F32),
        V((4, 8, R), F32), V((4, 4, 8, R), F32), V((LEN, 128), F32),
        V((4, R, COLS), BF16), V((4, R, COLS), BF16), V((LEN, COLS), BF16),
        V((LEN, COLS), F32), V((LEN, COLS), F32), V((LEN, COLS), F32), V((6, R, R), F32), V((4, LEN, COLS), BF16),
        V((2, R, 512), BF16), V((2, R, 512), BF16), V((2, 2, R, 512), BF16), V((2, 2, R, 512), BF16), V((R, D), F32),
        V((512, 512), BF16), V((512, 512), BF16),
        V((2, 4, 128, D), BF16), V((2, 4, 128, D), BF16), V((2, 4, 128, D), BF16),
        V((2, 16, 32, D), BF16), V((2, 16, 32, D), BF16), V((2, 32, D), F32), V((2, 4, 8, D), F32),
        V((8, 128), F32), V((8, 128), F32), V((16, 8, 128), F32), V((8, 128), F32), V((4, 8, 128), F32),
        dma((5,)), dma((32,)), dma((32,)), dma((4,)), dma((4,)), dma((2, 4)), dma((2, 4)), dma((4,)), dma((4,)),
        dma((4,)), dma((4,)), dma((4,)), dma((4,)),
        dma((2,)), dma((2,)), dma((2, 2)), dma((2, 2)), dma((32,)), dma((32,)),
        dma((2, 4)), dma((2, 4)), dma((2, 16)), dma((2, 16)), dma((2, 4)), dma((2, 4)),
        dma(()), dma(()), dma((16,)), dma((16,)), dma((4,)), dma((4,)),
    ]
    outs = pl.pallas_call(
        kernel,
        out_shape=(
            jax.ShapeDtypeStruct((R, D), BF16),
            jax.ShapeDtypeStruct((R, D), BF16),
            jax.ShapeDtypeStruct((8, 4 * D), F32),
            jax.ShapeDtypeStruct((8, D), F32),
            jax.ShapeDtypeStruct((8, 128), F32),
        ),
        in_specs=[vmem, vmem, smem, hbm, hbm, smem, vmem],
        out_specs=(vmem,) * 5,
        scratch_shapes=scratch,
        compiler_params=pltpu.CompilerParams(
            collective_id=0, has_side_effects=True, vmem_limit_bytes=60 * 1024 * 1024
        ),
        name="hstu_layer",
    )(tokens, send_rows, user_lengths, input_weight, output_weight, distance_bias, upstream)
    return outs[0], outs[1], outs[2], outs[3], outs[4][:, :NB]


def solution(mesh):
    block = P(("dp", "ctx"), None)
    in_specs = (block, block, P("dp", None), P(), P(), P(), block)
    out_specs = (block, block, block, block, P())
    return jax.shard_map(shards, mesh=mesh, in_specs=in_specs, out_specs=out_specs, check_vma=False)
```

```python
import jax
import jax.numpy as jnp
from jax import lax
from jax.experimental import pallas as pl
from jax.experimental.pallas import tpu as pltpu
from jax.sharding import PartitionSpec as P

PLANES = (0, 1, 3, 2)
AHEAD = 3

H = 8
DH = 128
NB = 12
N_CTX = 4
R = 256
D = 1024
LEN = 1024
COLS = 256
HEADS = 2
EPSILON = 1e-05
HIDDEN = -(2.0**40)
SCALE = DH ** (-0.5)
F32 = jnp.float32
BF16 = jnp.bfloat16
MESH = pl.DeviceIdType.MESH
NN = ((1,), (0,))
NT = ((1,), (1,))
TN = ((0,), (0,))


def dot(left, right, dims):
    return lax.dot_general(left, right, (dims, ((), ())), preferred_element_type=F32)


def at(start, size):
    return pl.ds(pl.multiple_of(start, size), size)


def silu_parts(halved):
    rise = 1.0 + jnp.tanh(halved)
    active = halved * rise
    return active, active + (0.5 * rise) * (1.0 - active)


def copy_to(src, dst, send_sem, recv_sem, dp, ctx):
    return pltpu.make_async_remote_copy(
        src_ref=src, dst_ref=dst, send_sem=send_sem, recv_sem=recv_sem, device_id=(dp, ctx), device_id_type=MESH
    )


def split_halves(rows):
    count = rows.shape[0] // 8
    left = rows[:, :512].reshape(count, 1, 8, 512)
    right = rows[:, 512:].reshape(count, 1, 8, 512)
    return jnp.concatenate((left, right), axis=1).reshape(count * 16, 512)


def join_halves(pairs):
    count = pairs.shape[0] // 16
    parts = pairs.reshape(count, 2, 8, 512)
    return jnp.concatenate((parts[:, 0].reshape(count * 8, 512), parts[:, 1].reshape(count * 8, 512)), axis=1)


def kernel(
    tokens, send_rows, lengths, weight_in, weight_out, bias_table, upstream,
    layer_output, token_gradient, input_gradient, output_gradient, bias_gradient,
    w_in, w_out, pick, message, balanced, unit, inverse_in, normed, gg_send, gg_all, slope, act, bias_tile,
    w_tile, s_tile, attended, stats_send, stats_all, rows_stat, gated, gated_all, att_grad, dq, dk, dv, bias_sum, pg, turned, q_user, k_user,
    ng_far, ng_far_in, ng_near, ng_near_in, ng_own, back, back_in,
    g_core, g_core_in, ga, ga_in, gb, gb_in, ha, ha_in, hb, hb_in, g_row, g_row_in,
    b_core, b_core_in, b_chip_in, b_row, b_row_in,
    w_sem, a_send, a_recv, gg_ssem, gg_rsem, z_send, z_recv, f_send, f_recv, st_send, st_recv, gt_send, gt_recv,
    nf_send, nf_recv, nn_send, nn_recv, r_send, r_recv, gc_send, gc_recv, ga_send, ga_recv, gb_send, gb_recv, ha_send, ha_recv, hb_send, hb_recv, gr_send, gr_recv,
    bc_send, bc_recv, bk_send, bk_recv, br_send, br_recv,
):
    me = lax.axis_index("dp")
    sent, due = [], {}
    def ring(n, base, fn):
        @pl.loop(1, n)
        def _(step):
            fn((base + step) % n)
    def take(key):
        due.pop(key)()
    ctx = lax.axis_index("ctx")
    plane, inner = me // 8, me % 8
    chip, core = me // 2, me % 2
    partner = chip * 2 + (1 - core)
    right, left, far = (ctx + 1) % 4, (ctx + 3) % 4, (ctx + 2) % 4
    x, y = chip // 4, chip % 4
    ordered = (ctx, right, left, far)

    out_copy = pltpu.make_async_copy(weight_out, w_out, w_sem.at[4])
    out_copy.start()
    in_copies = []
    for part in range(4):
        columns = pl.ds(pl.multiple_of(part * D + ctx * COLS, COLS), COLS)
        in_copies.append(pltpu.make_async_copy(weight_in.at[:, columns], w_in.at[:, pl.ds(part * COLS, COLS)], w_sem.at[part]))
        in_copies[-1].start()
    due["w4"] = out_copy.wait
    for part in range(4):
        due["w%d" % part] = in_copies[part].wait

    barrier = pltpu.get_barrier_semaphore()

    @pl.loop(1, 32)
    def _(step):
        pl.semaphore_signal(barrier, inc=1, device_id=((me + step) % 32, ctx), device_id_type=MESH)

    for step in range(1, 4):
        pl.semaphore_signal(barrier, inc=1, device_id=(me, (ctx + step) % 4), device_id_type=MESH)

    rows_of = lax.broadcasted_iota(jnp.int32, (R, R), 0)
    pick[...] = jnp.where(rows_of == send_rows[...], 1.0, 0.0).astype(BF16)
    message[...] = split_halves(dot(pick[...], tokens[...], TN)).astype(BF16)

    pl.semaphore_wait(barrier, 34)

    def token_copy(dst):
        return copy_to(
            message.at[at(dst * 16, 16), :], balanced.at[at(me * 16, 16), :], a_send.at[dst], a_recv.at[me], dst, ctx
        )

    def token_arrival(src):
        return copy_to(
            message.at[at(src * 16, 16), :], balanced.at[at(src * 16, 16), :], a_send.at[src], a_recv.at[src], src, ctx
        )

    def send_plane(p):
        @pl.loop(1 if p == 0 else 0, 8)
        def _(q):
            token_copy((plane + p) % 4 * 8 + (inner + q) % 8).start()

    for p in PLANES[:AHEAD]:
        send_plane(p)
    balanced[at(me * 16, 16), :] = message[at(me * 16, 16), :]
    sent.append(lambda: ring(32, me, lambda o: token_copy(o).wait_send()))

    take("w4")

    def gg_copy(block):
        return copy_to(
            gg_send.at[block], gg_all.at[ctx], gg_ssem.at[block], gg_rsem.at[ctx], me, block
        )

    for step in (2, 1, 3, 0):
        block = (ctx + step) % 4
        result = dot(upstream[...], w_out[at(block * COLS, COLS), :], NT).astype(BF16)
        if step == 0:
            gg_all[ctx] = result
        else:
            gg_send[block] = result
            gg_copy(block).start()
            sent.append(lambda block=block: gg_copy(block).wait_send())
            due["gg%d" % step] = lambda block=block: copy_to(gg_send.at[block], gg_all.at[block], gg_ssem.at[block], gg_rsem.at[block], me, block).wait_recv()

    def near_copy(p, side):
        rows = at(ctx * R + (plane + 4 - p) % 4 * 64, 64)
        return copy_to(
            normed.at[rows, :], normed.at[rows, :], z_send.at[side, p], z_recv.at[side, p], me, right if side == 0 else left
        )

    def near_arrival(p, side):
        rows = at((left if side == 0 else right) * R + (plane + 4 - p) % 4 * 64, 64)
        return copy_to(
            normed.at[rows, :], normed.at[rows, :], z_send.at[side, p], z_recv.at[side, p], me, right if side == 0 else left
        )

    def far_copy(p, side):
        rows = at((left if side == 0 else right) * R + (plane + 4 - p) % 4 * 64, 64)
        return copy_to(
            normed.at[rows, :], normed.at[rows, :], f_send.at[p], f_recv.at[p], me, right if side == 0 else left
        )

    def far_arrival(p, side):
        rows = at(far * R + (plane + 4 - p) % 4 * 64, 64)
        return copy_to(
            normed.at[rows, :], normed.at[rows, :], f_send.at[p], f_recv.at[p], me, right if side == 0 else left
        )

    for order, p in enumerate(PLANES):
        source = (plane + 4 - p) % 4

        @pl.loop(1 if p == 0 else 0, 8)
        def _(q):
            token_arrival(source * 8 + (inner + 8 - q) % 8).wait_recv()

        if order + AHEAD < 4:
            send_plane(PLANES[order + AHEAD])
        rows = join_halves(balanced[at(source * 128, 128), :].astype(F32))
        mean = jnp.mean(rows, axis=1, keepdims=True)
        centered = rows - mean
        inverse = lax.rsqrt(jnp.mean(centered * centered, axis=1, keepdims=True) + EPSILON)
        values = centered * inverse
        unit[at(source * 64, 64), :] = values
        inverse_in[at(source * 64, 64), :] = jnp.broadcast_to(inverse, (64, 128))
        normed[at(ctx * R + source * 64, 64), :] = values.astype(BF16)
        for side in range(2):
            near_copy(p, side).start()
            sent.append(lambda p=p, side=side: near_copy(p, side).wait_send())
            due["n%d%d" % (p, side)] = lambda p=p, side=side: near_arrival(p, side).wait_recv()

    for part in range(4):
        take("w%d" % part)

    attended[...] = jnp.zeros((LEN, COLS), F32)
    dq[...] = jnp.zeros((LEN, COLS), F32)
    dk[...] = jnp.zeros((LEN, COLS), F32)
    dv[...] = jnp.zeros((LEN, COLS), F32)
    bias_sum[...] = jnp.zeros((6, R, R), F32)

    end_0 = lengths[0, 0]
    end_1 = end_0 + lengths[0, 1]
    position = lax.broadcasted_iota(jnp.int32, (LEN, DH), 0)
    user = jnp.where(position >= end_0, 1, 0) + jnp.where(position >= end_1, 1, 0)
    same = user == lax.broadcasted_iota(jnp.int32, (LEN, DH), 1)
    q_user[...] = jnp.where(same, 1.0, 0.0).astype(BF16)
    k_user[...] = jnp.where(same, 0.0, HIDDEN).astype(BF16)

    def project(block):
        rows = at(block * R, R)
        for part in range(4):
            active, rate = silu_parts(0.5 * dot(normed[rows, :], w_in[:, part * COLS : part * COLS + COLS], NN))
            act[part, rows, :] = active.astype(BF16)
            slope[part, rows, :] = rate

    for p in PLANES[:2]:
        take("n%d%d" % (p, 0))
        far_copy(p, 0).start()
        sent.append(lambda p=p: far_copy(p, 0).wait_send())
        due["f%d%d" % (p, 0)] = lambda p=p: far_arrival(p, 0).wait_recv()

    for hh in range(HEADS):
        for r in range(3):
            reach = (
                lax.broadcasted_iota(jnp.int32, (R, R), 0) - lax.broadcasted_iota(jnp.int32, (R, R), 1) + (r * R + 1)
            )
            low, high = ((0, 8), (1, 9), (8, 9))[r]
            tile = jnp.full((R, R), 0.5 * bias_table[ctx * HEADS + hh, low], F32)
            for level in range(low + 1, high + 1):
                tile = jnp.where(reach >= 2**level, 0.5 * bias_table[ctx * HEADS + hh, level], tile)
            if r == 0:
                tile = jnp.where(reach >= 1, tile, HIDDEN)
            bias_tile[hh * 3 + r] = tile

    def pairs(place, body):
        @pl.loop(0, place + 1)
        def _(other):
            a = ordered[place]
            b = (ctx + other + other // 2 - 2 * (other // 3)) % 4
            a_last = (a - b + 4) // 4
            q = b + (a - b) * a_last
            k = a + b - q
            r = q - k

            @pl.when(r < 3)
            def _():
                body(q, k, r, q + 3 * r - r // 2)

    def attend(q, k, r, slot):
        q_rows, k_rows = at(q * R, R), at(k * R, R)
        for hh in range(HEADS):
            cols = slice(hh * DH, hh * DH + DH)
            query = jnp.concatenate((act[2, q_rows, cols], q_user[q_rows, :]), axis=1)
            keys = jnp.concatenate((act[3, k_rows, cols], k_user[k_rows, :]), axis=1)
            active, rate = silu_parts(dot(query, keys, NT) * (0.5 * SCALE) + bias_tile[hh * 3 + r])
            weights = active.astype(BF16)
            s_tile[hh, slot] = rate
            w_tile[hh, slot] = weights
            attended[q_rows, cols] += dot(weights, act[1, k_rows, cols], NN)

    project(ctx)
    for p in PLANES[2:]:
        take("n%d%d" % (p, 1))
        far_copy(p, 1).start()
        sent.append(lambda p=p: far_copy(p, 1).wait_send())
        due["f%d%d" % (p, 1)] = lambda p=p: far_arrival(p, 1).wait_recv()
    pairs(0, attend)
    for p in PLANES[:2]:
        take("n%d%d" % (p, 1))
    project(right)
    pairs(1, attend)
    for p in PLANES[2:]:
        take("n%d%d" % (p, 0))
    project(left)
    pairs(2, attend)
    for order, p in enumerate(PLANES):
        take("f%d%d" % (p, order // 2))
    project(far)
    pairs(3, attend)

    for step in range(1, 4):
        take("gg%d" % step)

    lane = lax.broadcasted_iota(jnp.int32, (R, 128), 1)

    @pl.loop(0, 4)
    def _(block):
        rows = attended[at(block * R, R), :]
        mean = jnp.mean(rows, axis=1, keepdims=True)
        centered = rows - mean
        flow = gg_all[block].astype(F32) * act[0, at(block * R, R), :].astype(F32)
        packed = jnp.where(lane == 0, mean, 0.0)
        packed = jnp.where(lane == 1, jnp.sum(centered * centered, axis=1, keepdims=True), packed)
        packed = jnp.where(lane == 2, jnp.sum(flow, axis=1, keepdims=True), packed)
        packed = jnp.where(lane == 3, jnp.sum(flow * centered, axis=1, keepdims=True), packed)
        stats_send[block] = packed.T[:8, :]

    def stats_copy(block):
        return copy_to(stats_send, stats_all.at[ctx], st_send.at[block], st_recv.at[ctx], me, block)

    for step in range(1, 4):
        stats_copy((ctx + step) % 4).start()
    stats_all[ctx] = stats_send[...]

    @pl.loop(0, 4)
    def _(piece):
        columns = at(piece * R, R)
        for b in range(4):
            turned[columns, b * R : b * R + R] = normed[b * R : b * R + R, columns].T

    for step in range(1, 4):
        block = (ctx + step) % 4
        sent.append(lambda block=block: stats_copy(block).wait_send())
        copy_to(stats_send, stats_all.at[block], st_send.at[block], st_recv.at[block], me, block).wait_recv()

    for block in range(4):
        parts = [stats_all[c, block] for c in range(4)]
        means = [x[0:1] for x in parts]
        mean = (means[0] + means[1] + means[2] + means[3]) * 0.25
        square = sum(parts[c][1:2] + COLS * (means[c] - mean) * (means[c] - mean) for c in range(4))
        flow = sum(parts[c][2:3] for c in range(4))
        cross = sum(parts[c][3:4] + (means[c] - mean) * parts[c][2:3] for c in range(4))
        inverse = lax.rsqrt(square * (1.0 / D) + EPSILON)
        table = jnp.concatenate(
            (mean, inverse, flow * (1.0 / D), cross * inverse * (1.0 / D), jnp.zeros((124, R), F32)), axis=0
        )
        rows_stat[pl.ds(block * R, R), :] = table.T

    def gated_copy(block):
        return copy_to(gated.at[block], gated_all.at[ctx], gt_send.at[block], gt_recv.at[ctx], me, block)

    @pl.loop(0, 4)
    def _(block):
        rows = at(block * R, R)
        table = rows_stat[rows, :]
        inverse = table[:, 1:2]
        out_unit = (attended[rows, :] - table[:, 0:1]) * inverse
        gate = act[0, rows, :].astype(F32)
        flow = gg_all[block].astype(F32)
        gated[block] = (out_unit * gate).astype(BF16)
        pg[rows, 0:COLS] = (flow * out_unit * slope[0, rows, :]).astype(BF16)
        att_grad[rows, :] = (inverse * (flow * gate - table[:, 2:3] - out_unit * table[:, 3:4])).astype(BF16)

    for step in range(1, 4):
        block = (ctx + step) % 4
        gated_copy(block).start()
        sent.append(lambda block=block: gated_copy(block).wait_send())
        due["gt%d" % step] = lambda block=block: copy_to(gated.at[block], gated_all.at[block], gt_send.at[block], gt_recv.at[block], me, block).wait_recv()
    gated_all[ctx] = gated[ctx]

    def core_copy(which, piece, half):
        cols = pl.ds(half * 512, 512)
        return copy_to(
            g_core.at[which, 1 - core, piece, :, cols], g_core_in.at[which, piece, :, cols], gc_send.at[which, piece, half],
            gc_recv.at[which, piece, half], partner, ctx,
        )

    def along_x(which, other):
        return copy_to(
            ga.at[which, other], ga_in.at[which, x], ga_send.at[which, other], ga_recv.at[which, x],
            (other * 4 + y) * 2 + core, ctx,
        )

    def from_x(which, other):
        return copy_to(
            ga.at[which, other], ga_in.at[which, other], ga_send.at[which, other], ga_recv.at[which, other],
            (other * 4 + y) * 2 + core, ctx,
        )

    def along_y(which, other):
        return copy_to(
            gb.at[which, other], gb_in.at[which, y], gb_send.at[which, other], gb_recv.at[which, y],
            (x * 4 + other) * 2 + core, ctx,
        )

    def from_y(which, other):
        return copy_to(
            gb.at[which, other], gb_in.at[which, other], gb_send.at[which, other], gb_recv.at[which, other],
            (x * 4 + other) * 2 + core, ctx,
        )

    def then_y(which, other):
        return copy_to(
            ha.at[which, other], ha_in.at[which, y], ha_send.at[which, other], ha_recv.at[which, y],
            (x * 4 + other) * 2 + core, ctx,
        )

    def then_from_y(which, other):
        return copy_to(
            ha.at[which, other], ha_in.at[which, other], ha_send.at[which, other], ha_recv.at[which, other],
            (x * 4 + other) * 2 + core, ctx,
        )

    def then_x(which, other):
        return copy_to(
            hb.at[which, other], hb_in.at[which, x], hb_send.at[which, other], hb_recv.at[which, x],
            (other * 4 + y) * 2 + core, ctx,
        )

    def then_from_x(which, other):
        return copy_to(
            hb.at[which, other], hb_in.at[which, other], hb_send.at[which, other], hb_recv.at[which, other],
            (other * 4 + y) * 2 + core, ctx,
        )

    def row_copy(which, block):
        return copy_to(
            g_row.at[which, at(block * 8, 8), :], g_row_in.at[which, ctx], gr_send.at[which, block],
            gr_recv.at[which, ctx], me, block,
        )

    def row_arrival(which, block):
        return copy_to(
            g_row.at[which, at(block * 8, 8), :], g_row_in.at[which, block], gr_send.at[which, block],
            gr_recv.at[which, block], me, block,
        )

    def keep_tile(which, piece, column, tile):
        halves = tile.reshape(4, 2, 32, COLS)
        first, second = halves[:, 0].reshape(128, COLS), halves[:, 1].reshape(128, COLS)
        cols = slice(column * COLS, column * COLS + COLS)
        g_core[which, 0, piece, :, cols] = first.astype(BF16)
        g_core[which, 1, piece, :, cols] = second.astype(BF16)

    def send_core(which, piece, half):
        core_copy(which, piece, half).start()
        sent.append(lambda: core_copy(which, piece, half).wait_send())
        due["gc%d%d%d" % (which, piece, half)] = lambda: core_copy(which, piece, half).wait_recv()

    def spread(which, half):
        cols = slice(half * 512, half * 512 + 512)
        for piece in range(4):
            take("gc%d%d%d" % (which, piece, half))
            both = g_core[which, core, piece, :, cols].astype(F32) + g_core_in[which, piece, :, cols].astype(F32)
            both = both.astype(BF16)
            if half == 0:
                ga[which, piece] = both.reshape(4, 32, 512)
            else:
                for row in range(4):
                    gb[which, row, piece] = both[row * 32 : row * 32 + 32]
        go, come, here = ((along_x, from_x, x), (along_y, from_y, y))[half]
        for step in (2, 1, 3):
            other = (here + step) % 4
            go(which, other).start()
            sent.append(lambda other=other: go(which, other).wait_send())
            due["g%d%d%d" % (half, which, step)] = lambda other=other: come(which, other).wait_recv()
        if half == 0:
            ga_in[which, x] = ga[which, x]
        else:
            gb_in[which, y] = gb[which, y]

    def spread_again(which, half):
        for step in (1, 3, 2):
            take("g%d%d%d" % (half, which, step))
        arrived, held, landed = ((ga_in, ha, ha_in), (gb_in, hb, hb_in))[half]
        total = arrived[which, 0].astype(F32)
        for other in range(1, 4):
            total = total + arrived[which, other].astype(F32)
        held[which] = total.astype(BF16)
        go, come, here = ((then_y, then_from_y, y), (then_x, then_from_x, x))[half]
        for step in (2, 1, 3):
            other = (here + step) % 4
            go(which, other).start()
            sent.append(lambda other=other: go(which, other).wait_send())
            due["h%d%d%d" % (half, which, step)] = lambda other=other: come(which, other).wait_recv()
        landed[which, here] = held[which, here]

    def finish_sum(which):
        for half in range(2):
            for step in (1, 3, 2):
                take("h%d%d%d" % (half, which, step))
            landed = (ha_in, hb_in)[half]
            total = landed[which, 0].astype(F32)
            for other in range(1, 4):
                total = total + landed[which, other].astype(F32)
            g_row[which, :, half * 512 : half * 512 + 512] = total
        for step in (2, 1, 3):
            block = (ctx + step) % 4
            row_copy(which, block).start()
            sent.append(lambda block=block: row_copy(which, block).wait_send())
            due["gr%d%d" % (which, step)] = lambda block=block: row_arrival(which, block).wait_recv()
        g_row_in[which, ctx] = g_row[which, at(ctx * 8, 8), :]

    def attend_back(q, k, r, slot):
        q_rows, k_rows = at(q * R, R), at(k * R, R)
        for hh in range(HEADS):
            cols = slice(hh * DH, hh * DH + DH)
            incoming = att_grad[q_rows, cols]
            change = dot(incoming, act[1, k_rows, cols], NT) * s_tile[hh, slot]
            bias_sum[hh * 3 + r] += change
            rounded = change.astype(BF16)
            dq[q_rows, cols] += dot(rounded, act[3, k_rows, cols], NN)
            dk[k_rows, cols] += dot(rounded, act[2, q_rows, cols], TN)
            dv[k_rows, cols] += dot(w_tile[hh, slot], incoming, TN)

    def close_block(block):
        rows = at(block * R, R)
        pg[rows, 1 * COLS : 1 * COLS + COLS] = (dv[rows, :] * slope[1, rows, :]).astype(BF16)
        pg[rows, 2 * COLS : 2 * COLS + COLS] = (dq[rows, :] * SCALE * slope[2, rows, :]).astype(BF16)
        pg[rows, 3 * COLS : 3 * COLS + COLS] = (dk[rows, :] * SCALE * slope[3, rows, :]).astype(BF16)

    def block_terms(block, half):
        rows = at(block * R, R)
        return dot(pg[rows, :], w_in[half * 512 : half * 512 + 512, :], NT)

    def far_part(side):
        return copy_to(
            ng_far.at[side], ng_far_in.at[side], nf_send.at[side], nf_recv.at[side], me, right if side == 0 else left
        )

    def near_part(side, half, p):
        rows = at((plane + p) % 4 * 64, 64)
        return copy_to(
            ng_near.at[side, half, rows, :], ng_near_in.at[side, half, rows, :], nn_send.at[side, half, p],
            nn_recv.at[side, half, p], me, right if side == 0 else left,
        )

    def send_near(side, half, p):
        near_part(side, half, p).start()
        sent.append(lambda: near_part(side, half, p).wait_send())
        due["nn%d%d%d" % (side, half, p)] = lambda: near_part(side, half, p).wait_recv()

    pairs(3, attend_back)
    close_block(far)
    for side in range(2):
        ng_far[side] = block_terms(far, side).astype(BF16)
        far_part(side).start()
        sent.append(lambda side=side: far_part(side).wait_send())
        due["nf%d" % side] = lambda side=side: far_part(side).wait_recv()

    for step in range(1, 4):
        take("gt%d" % step)
    for piece in range(4):
        left_rows = gated_all[piece].T

        for column in range(4):
            keep_tile(1, piece, column, dot(left_rows, upstream[:, column * COLS : column * COLS + COLS], NN))

        send_core(1, piece, 0)
        send_core(1, piece, 1)

    for place, side in ((2, 1), (1, 0)):
        pairs(place, attend_back)
        block = ordered[place]
        close_block(block)
        ng_near[side, 1 - side] = block_terms(block, 1 - side).astype(BF16)
        for p in PLANES:
            send_near(side, 1 - side, p)
    spread(1, 0)
    spread(1, 1)
    pairs(0, attend_back)
    close_block(ctx)

    def input_half(half):
        for piece in range(4):
            for part in range(half * 2, half * 2 + 2):
                cols = slice(part * COLS, part * COLS + COLS)
                keep_tile(0, piece, part, dot(turned[piece * R : piece * R + R, :], pg[:, cols], NN))

            send_core(0, piece, half)

    input_half(0)
    for side in range(2):
        terms = block_terms(right if side == 0 else left, side)
        take("nf%d" % side)
        ng_near[side, side] = (terms + ng_far_in[side].astype(F32)).astype(BF16)
    for p in PLANES:
        for side in range(2):
            send_near(side, side, p)
    spread(0, 0)
    input_half(1)
    spread_again(1, 0)
    spread_again(1, 1)
    spread(0, 1)
    for half in range(2):
        ng_own[:, half * 512 : half * 512 + 512] = block_terms(ctx, half)

    for half in range(2):
        cols = slice(half * 512, half * 512 + 512)
        total = dot(gated_all[0], w_out[0:COLS, cols], NN)
        for c in range(1, 4):
            total = total + dot(gated_all[c], w_out[c * COLS : c * COLS + COLS, cols], NN)
        pairs = balanced[...].astype(F32).reshape(32, 2, 8, 512)
        layer_output[:, cols] = (pairs[:, half].reshape(R, 512) + total).astype(BF16)

    sums = jnp.zeros((8, 128), F32)
    tile_row = lax.broadcasted_iota(jnp.int32, (8, 128), 0)
    tile_lane = lax.broadcasted_iota(jnp.int32, (8, 128), 1)
    for hh in range(HEADS):
        for r in range(3):
            reach = (
                lax.broadcasted_iota(jnp.int32, (R, R), 0) - lax.broadcasted_iota(jnp.int32, (R, R), 1) + (r * R + 1)
            )
            low, high = ((0, 8), (1, 9), (8, 9))[r]
            tile = bias_sum[hh * 3 + r]
            for level in range(low, high + 1):
                part = tile
                if level > low:
                    part = jnp.where(reach >= 2**level, part, 0.0)
                if level < high:
                    part = jnp.where(reach < 2 ** (level + 1), part, 0.0)
                total = jnp.sum(jnp.sum(part, axis=0, keepdims=True), axis=1, keepdims=True)
                place = jnp.logical_and(tile_row == ctx * HEADS + hh, tile_lane == level)
                sums = sums + jnp.where(place, total, 0.0)
    b_core[...] = sums
    bias_core = copy_to(b_core, b_core_in, bc_send, bc_recv, partner, ctx)
    bias_core.start()
    sent.append(lambda: bias_core.wait_send())
    due["bc"] = lambda: bias_core.wait_recv()


    def back_copy(dst):
        return copy_to(
            back.at[at(dst * 16, 16), :], back_in.at[at(me * 16, 16), :], r_send.at[dst], r_recv.at[me], dst, ctx
        )

    def back_arrival(src):
        return copy_to(
            back.at[at(src * 16, 16), :], back_in.at[at(src * 16, 16), :], r_send.at[src], r_recv.at[src], src, ctx
        )

    for order, p in enumerate(PLANES):
        if order > 1:
            spread_again(0, order - 2)
        for side in range(2):
            for half in range(2):
                take("nn%d%d%d" % (side, half, p))
        target = (plane + p) % 4
        rows = at(target * 64, 64)
        total = []
        for half in range(2):
            total.append(
                ng_own[rows, half * 512 : half * 512 + 512]
                + ng_near_in[0, half, rows, :].astype(F32)
                + ng_near_in[1, half, rows, :].astype(F32)
            )
        total = jnp.concatenate(total, axis=1)
        values = unit[rows, :]
        plain = jnp.mean(total, axis=1, keepdims=True)
        cross = jnp.mean(total * values, axis=1, keepdims=True)
        change = inverse_in[rows, 0:1] * (total - plain - values * cross)
        result = upstream[rows, :].astype(F32) + change
        back[at(target * 128, 128), :] = split_halves(result).astype(BF16)

        @pl.loop(1 if p == 0 else 0, 8)
        def _(q):
            back_copy(target * 8 + (inner + q) % 8).start()

    back_in[at(me * 16, 16), :] = back[at(me * 16, 16), :]
    sent.append(lambda: ring(32, me, lambda o: back_copy(o).wait_send()))
    due["back"] = lambda: ring(32, me, lambda o: back_arrival(o).wait_recv())

    take("bc")
    b_chip_in[chip] = b_core[...] + b_core_in[...]

    def bias_chip(other):
        return copy_to(
            b_chip_in.at[chip], b_chip_in.at[chip], bk_send.at[other], bk_recv.at[chip], other * 2 + core, ctx
        )

    @pl.loop(1, 16)
    def _(step):
        bias_chip((chip + step) % 16).start()

    sent.append(lambda: ring(16, chip, lambda o: bias_chip(o).wait_send()))
    due["bk"] = lambda: ring(16, chip, lambda other: copy_to(
            b_chip_in.at[other], b_chip_in.at[other], bk_send.at[other], bk_recv.at[other], other * 2 + core, ctx
        ).wait_recv())
    finish_sum(1)
    finish_sum(0)
    take("bk")

    total = b_chip_in[0]
    for other in range(1, 16):
        total = total + b_chip_in[other]
    b_row[...] = total
    b_row_in[ctx] = total
    for step in range(1, 4):
        block = (ctx + step) % 4
        copy_to(b_row, b_row_in.at[ctx], br_send.at[block], br_recv.at[ctx], me, block).start()
        sent.append(lambda block=block: copy_to(b_row, b_row_in.at[ctx], br_send.at[block], br_recv.at[ctx], me, block).wait_send())

    take("back")

    returned = join_halves(back_in[...].astype(F32)).astype(BF16)
    token_gradient[...] = dot(pick[...], returned, NN).astype(BF16)

    for step in range(1, 4):
        block = (ctx + step) % 4
        take("gr0%d" % step)
        take("gr1%d" % step)
        copy_to(b_row, b_row_in.at[block], br_send.at[block], br_recv.at[block], me, block).wait_recv()
    for c in range(4):
        for part in range(4):
            input_gradient[:, part * D + c * COLS : part * D + c * COLS + COLS] = g_row_in[
                0, c, :, part * COLS : part * COLS + COLS
            ]
    output_gradient[...] = g_row_in[1, 0] + g_row_in[1, 1] + g_row_in[1, 2] + g_row_in[1, 3]
    bias_gradient[...] = (b_row_in[0] + b_row_in[1] + b_row_in[2] + b_row_in[3])[:, :NB]

    for fn in sent:
        fn()


def hand_over(*refs):
    for source, target in zip(refs[:5], refs[5:]):
        target[...] = source[...]


def shards(tokens, send_rows, user_lengths, input_weight, output_weight, distance_bias, upstream):
    vmem = pl.BlockSpec(memory_space=pltpu.VMEM)
    smem = pl.BlockSpec(memory_space=pltpu.SMEM)
    hbm = pl.BlockSpec(memory_space=pl.ANY)
    dma = pltpu.SemaphoreType.DMA
    V = pltpu.VMEM
    scratch = [
        V((D, D), BF16), V((D, D), BF16), V((R, R), BF16), V((512, 512), BF16), V((512, 512), BF16),
        V((R, D), F32), V((R, 128), F32), V((LEN, D), BF16), V((4, R, COLS), BF16), V((4, R, COLS), BF16),
        V((4, LEN, COLS), F32), V((4, LEN, COLS), BF16), V((6, R, R), F32),
        V((HEADS, 9, R, R), BF16), V((HEADS, 9, R, R), F32), V((LEN, COLS), F32),
        V((4, 8, R), F32), V((4, 4, 8, R), F32), V((LEN, 128), F32),
        V((4, R, COLS), BF16), V((4, R, COLS), BF16), V((LEN, COLS), BF16),
        V((LEN, COLS), F32), V((LEN, COLS), F32), V((LEN, COLS), F32), V((6, R, R), F32), V((LEN, D), BF16), V((D, LEN), BF16),
        V((LEN, DH), BF16), V((LEN, DH), BF16),
        V((2, R, 512), BF16), V((2, R, 512), BF16), V((2, 2, R, 512), BF16), V((2, 2, R, 512), BF16), V((R, D), F32),
        V((512, 512), BF16), V((512, 512), BF16),
        V((2, 2, 4, 128, D), BF16), V((2, 4, 128, D), BF16),
        V((2, 4, 4, 32, 512), BF16), V((2, 4, 4, 32, 512), BF16), V((2, 4, 4, 32, 512), BF16),
        V((2, 4, 4, 32, 512), BF16), V((2, 4, 32, 512), BF16), V((2, 4, 32, 512), BF16),
        V((2, 4, 32, 512), BF16), V((2, 4, 32, 512), BF16), V((2, 32, D), F32), V((2, 4, 8, D), F32),
        V((8, 128), F32), V((8, 128), F32), V((16, 8, 128), F32), V((8, 128), F32), V((4, 8, 128), F32),
        dma((5,)), dma((32,)), dma((32,)), dma((4,)), dma((4,)), dma((2, 4)), dma((2, 4)), dma((4,)), dma((4,)),
        dma((4,)), dma((4,)), dma((4,)), dma((4,)),
        dma((2,)), dma((2,)), dma((2, 2, 4)), dma((2, 2, 4)), dma((32,)), dma((32,)),
        dma((2, 4, 2)), dma((2, 4, 2)), dma((2, 4)), dma((2, 4)), dma((2, 4)), dma((2, 4)), dma((2, 4)), dma((2, 4)),
        dma((2, 4)), dma((2, 4)), dma((2, 4)), dma((2, 4)),
        dma(()), dma(()), dma((16,)), dma((16,)), dma((4,)), dma((4,)),
    ]
    outs = pl.pallas_call(
        kernel,
        out_shape=(
            jax.ShapeDtypeStruct((R, D), BF16),
            jax.ShapeDtypeStruct((R, D), BF16),
            jax.ShapeDtypeStruct((8, 4 * D), F32),
            jax.ShapeDtypeStruct((8, D), F32),
            jax.ShapeDtypeStruct((8, NB), F32),
        ),
        in_specs=[vmem, vmem, smem, hbm, hbm, smem, vmem],
        out_specs=(vmem,) * 5,
        scratch_shapes=scratch,
        compiler_params=pltpu.CompilerParams(
            collective_id=0, has_side_effects=True, vmem_limit_bytes=60 * 1024 * 1024
        ),
        name="hstu_layer",
    )(tokens, send_rows, user_lengths, input_weight, output_weight, distance_bias, upstream)
    return pl.pallas_call(
        hand_over,
        out_shape=tuple(jax.ShapeDtypeStruct(o.shape, o.dtype) for o in outs),
        in_specs=[vmem] * 5,
        out_specs=(vmem,) * 5,
        name="results",
    )(*outs)


def solution(mesh):
    block = P(("dp", "ctx"), None)
    in_specs = (block, block, P("dp", None), P(), P(), P(), block)
    out_specs = (block, block, block, block, P())
    return jax.shard_map(shards, mesh=mesh, in_specs=in_specs, out_specs=out_specs, check_vma=False)
```

```python
import jax
import jax.numpy as jnp
from jax import lax
from jax.experimental import pallas as pl
from jax.experimental.pallas import tpu as pltpu
from jax.sharding import PartitionSpec as P

PLANES = (0, 1, 3, 2)
AHEAD = 3

H = 8
DH = 128
NB = 12
N_CTX = 4
R = 256
D = 1024
LEN = 1024
COLS = 256
HEADS = 2
EPSILON = 1e-05
HIDDEN = -(2.0**40)
SCALE = DH ** (-0.5)
F32 = jnp.float32
BF16 = jnp.bfloat16
MESH = pl.DeviceIdType.MESH
NN = ((1,), (0,))
NT = ((1,), (1,))
TN = ((0,), (0,))


def dot(left, right, dims):
    return lax.dot_general(left, right, (dims, ((), ())), preferred_element_type=F32)


def at(start, size):
    return pl.ds(pl.multiple_of(start, size), size)


def silu_parts(halved):
    rise = 1.0 + jnp.tanh(halved)
    active = halved * rise
    gate = 0.5 * rise
    return active, gate + active * (1.0 - gate)


def copy_to(src, dst, send_sem, recv_sem, dp, ctx):
    return pltpu.make_async_remote_copy(
        src_ref=src, dst_ref=dst, send_sem=send_sem, recv_sem=recv_sem, device_id=(dp, ctx), device_id_type=MESH
    )


def split_halves(rows):
    count = rows.shape[0] // 8
    left = rows[:, :512].reshape(count, 1, 8, 512)
    right = rows[:, 512:].reshape(count, 1, 8, 512)
    return jnp.concatenate((left, right), axis=1).reshape(count * 16, 512)


def join_halves(pairs):
    count = pairs.shape[0] // 16
    parts = pairs.reshape(count, 2, 8, 512)
    return jnp.concatenate((parts[:, 0].reshape(count * 8, 512), parts[:, 1].reshape(count * 8, 512)), axis=1)


def kernel(
    tokens, send_rows, lengths, weight_in, weight_out, bias_table, upstream,
    layer_output, token_gradient, input_gradient, output_gradient, bias_gradient,
    w_in, w_out, pick, message, balanced, unit, inverse_in, normed, gg_send, gg_all, slope, act, bias_tile,
    w_tile, s_tile, attended, stats_send, stats_all, rows_stat, gated, gated_all, att_grad, dq, dk, dv, bias_sum, pg, turned, q_user, k_user,
    ng_far, ng_far_in, ng_near, ng_near_in, ng_own, back, back_in,
    g_core, g_core_in, ga, ga_in, gb, gb_in, ha, ha_in, hb, hb_in, g_row, g_row_in,
    b_core, b_core_in, b_chip_in, b_row, b_row_in,
    w_sem, a_send, a_recv, gg_ssem, gg_rsem, z_send, z_recv, f_send, f_recv, st_send, st_recv, gt_send, gt_recv,
    nf_send, nf_recv, nn_send, nn_recv, r_send, r_recv, gc_send, gc_recv, ga_send, ga_recv, gb_send, gb_recv, ha_send, ha_recv, hb_send, hb_recv, gr_send, gr_recv,
    bc_send, bc_recv, bk_send, bk_recv, br_send, br_recv,
):
    me = lax.axis_index("dp")
    sent, due = [], {}
    def ring(n, base, fn):
        @pl.loop(1, n)
        def _(step):
            fn((base + step) % n)
    def take(key):
        due.pop(key)()
    ctx = lax.axis_index("ctx")
    plane, inner = me // 8, me % 8
    chip, core = me // 2, me % 2
    partner = chip * 2 + (1 - core)
    right, left, far = (ctx + 1) % 4, (ctx + 3) % 4, (ctx + 2) % 4
    x, y = chip // 4, chip % 4
    ordered = (ctx, right, left, far)

    barrier = pltpu.get_barrier_semaphore()

    @pl.loop(1, 32)
    def _(step):
        pl.semaphore_signal(barrier, inc=1, device_id=((me + step) % 32, ctx), device_id_type=MESH)

    for step in range(1, 4):
        pl.semaphore_signal(barrier, inc=1, device_id=(me, (ctx + step) % 4), device_id_type=MESH)

    out_copy = pltpu.make_async_copy(weight_out, w_out, w_sem.at[4])
    out_copy.start()
    in_copies = []
    for part in range(4):
        columns = pl.ds(pl.multiple_of(part * D + ctx * COLS, COLS), COLS)
        in_copies.append(pltpu.make_async_copy(weight_in.at[:, columns], w_in.at[:, pl.ds(part * COLS, COLS)], w_sem.at[part]))
        in_copies[-1].start()
    due["w4"] = out_copy.wait
    for part in range(4):
        due["w%d" % part] = in_copies[part].wait

    rows_of = lax.broadcasted_iota(jnp.int32, (R, R), 0)
    pick[...] = jnp.where(rows_of == send_rows[...], 1.0, 0.0).astype(BF16)
    message[...] = split_halves(dot(pick[...], tokens[...], TN)).astype(BF16)

    take("w4")

    def gg_copy(block):
        return copy_to(
            gg_send.at[block], gg_all.at[ctx], gg_ssem.at[block], gg_rsem.at[ctx], me, block
        )

    for block in range(4):
        gg_send[block] = dot(upstream[...], w_out[block * COLS : block * COLS + COLS, :], NT).astype(BF16)

    pl.semaphore_wait(barrier, 34)

    def token_copy(dst):
        return copy_to(
            message.at[at(dst * 16, 16), :], balanced.at[at(me * 16, 16), :], a_send.at[dst], a_recv.at[me], dst, ctx
        )

    def token_arrival(src):
        return copy_to(
            message.at[at(src * 16, 16), :], balanced.at[at(src * 16, 16), :], a_send.at[src], a_recv.at[src], src, ctx
        )

    def send_plane(p):
        @pl.loop(1 if p == 0 else 0, 8)
        def _(q):
            token_copy((plane + p) % 4 * 8 + (inner + q) % 8).start()

    for p in PLANES[:AHEAD]:
        send_plane(p)
    balanced[at(me * 16, 16), :] = message[at(me * 16, 16), :]
    sent.append(lambda: ring(32, me, lambda o: token_copy(o).wait_send()))

    for step in (2, 1, 3):
        block = (ctx + step) % 4
        gg_copy(block).start()
        sent.append(lambda block=block: gg_copy(block).wait_send())
        due["gg%d" % step] = lambda block=block: copy_to(
            gg_send.at[block], gg_all.at[block], gg_ssem.at[block], gg_rsem.at[block], me, block
        ).wait_recv()
    gg_all[ctx] = gg_send[ctx]

    def near_copy(p, side):
        rows = at(ctx * R + (plane + 4 - p) % 4 * 64, 64)
        return copy_to(
            normed.at[rows, :], normed.at[rows, :], z_send.at[side, p], z_recv.at[side, p], me, right if side == 0 else left
        )

    def near_arrival(p, side):
        rows = at((left if side == 0 else right) * R + (plane + 4 - p) % 4 * 64, 64)
        return copy_to(
            normed.at[rows, :], normed.at[rows, :], z_send.at[side, p], z_recv.at[side, p], me, right if side == 0 else left
        )

    def far_copy(p, side):
        rows = at((left if side == 0 else right) * R + (plane + 4 - p) % 4 * 64, 64)
        return copy_to(
            normed.at[rows, :], normed.at[rows, :], f_send.at[p], f_recv.at[p], me, right if side == 0 else left
        )

    def far_arrival(p, side):
        rows = at(far * R + (plane + 4 - p) % 4 * 64, 64)
        return copy_to(
            normed.at[rows, :], normed.at[rows, :], f_send.at[p], f_recv.at[p], me, right if side == 0 else left
        )

    for order, p in enumerate(PLANES):
        source = (plane + 4 - p) % 4

        @pl.loop(1 if p == 0 else 0, 8)
        def _(q):
            token_arrival(source * 8 + (inner + 8 - q) % 8).wait_recv()

        if order + AHEAD < 4:
            send_plane(PLANES[order + AHEAD])
        rows = join_halves(balanced[at(source * 128, 128), :].astype(F32))
        mean = jnp.mean(rows, axis=1, keepdims=True)
        centered = rows - mean
        inverse = lax.rsqrt(jnp.mean(centered * centered, axis=1, keepdims=True) + EPSILON)
        values = centered * inverse
        unit[at(source * 64, 64), :] = values
        inverse_in[at(source * 64, 64), :] = jnp.broadcast_to(inverse, (64, 128))
        normed[at(ctx * R + source * 64, 64), :] = values.astype(BF16)
        for side in range(2):
            near_copy(p, side).start()
            sent.append(lambda p=p, side=side: near_copy(p, side).wait_send())
            due["n%d%d" % (p, side)] = lambda p=p, side=side: near_arrival(p, side).wait_recv()

    for part in range(4):
        take("w%d" % part)

    attended[...] = jnp.zeros((LEN, COLS), F32)
    dq[...] = jnp.zeros((LEN, COLS), F32)
    dk[...] = jnp.zeros((LEN, COLS), F32)
    dv[...] = jnp.zeros((LEN, COLS), F32)
    bias_sum[...] = jnp.zeros((6, R, R), F32)

    end_0 = lengths[0, 0]
    end_1 = end_0 + lengths[0, 1]
    position = lax.broadcasted_iota(jnp.int32, (LEN, DH), 0)
    user = jnp.where(position >= end_0, 1, 0) + jnp.where(position >= end_1, 1, 0)
    same = user == lax.broadcasted_iota(jnp.int32, (LEN, DH), 1)
    q_user[...] = jnp.where(same, 1.0, 0.0).astype(BF16)
    k_user[...] = jnp.where(same, 0.0, HIDDEN).astype(BF16)

    def project(block):
        rows = at(block * R, R)
        for half in range(2):
            active, rate = silu_parts(0.5 * dot(normed[rows, :], w_in[:, half * 512 : half * 512 + 512], NN))
            for part in range(2):
                cols = slice(part * COLS, part * COLS + COLS)
                act[half * 2 + part, rows, :] = active[:, cols].astype(BF16)
                slope[half * 2 + part, rows, :] = rate[:, cols]

    for p in PLANES[:2]:
        take("n%d%d" % (p, 0))
        far_copy(p, 0).start()
        sent.append(lambda p=p: far_copy(p, 0).wait_send())
        due["f%d%d" % (p, 0)] = lambda p=p: far_arrival(p, 0).wait_recv()

    for hh in range(HEADS):
        for r in range(3):
            reach = (
                lax.broadcasted_iota(jnp.int32, (R, R), 0) - lax.broadcasted_iota(jnp.int32, (R, R), 1) + (r * R + 1)
            )
            low, high = ((0, 8), (1, 9), (8, 9))[r]
            tile = jnp.full((R, R), 0.5 * bias_table[ctx * HEADS + hh, low], F32)
            for level in range(low + 1, high + 1):
                tile = jnp.where(reach >= 2**level, 0.5 * bias_table[ctx * HEADS + hh, level], tile)
            if r == 0:
                tile = jnp.where(reach >= 1, tile, HIDDEN)
            bias_tile[hh * 3 + r] = tile

    def pairs(place, body):
        @pl.loop(0, place + 1)
        def _(other):
            a = ordered[place]
            b = (ctx + other + other // 2 - 2 * (other // 3)) % 4
            a_last = (a - b + 4) // 4
            q = b + (a - b) * a_last
            k = a + b - q
            r = q - k

            @pl.when(r < 3)
            def _():
                body(q, k, r, q + 3 * r - r // 2)

    def attend(q, k, r, slot):
        q_rows, k_rows = at(q * R, R), at(k * R, R)
        for hh in range(HEADS):
            cols = slice(hh * DH, hh * DH + DH)
            query = jnp.concatenate((act[2, q_rows, cols], q_user[q_rows, :]), axis=1)
            keys = jnp.concatenate((act[3, k_rows, cols], k_user[k_rows, :]), axis=1)
            active, rate = silu_parts(dot(query, keys, NT) * (0.5 * SCALE) + bias_tile[hh * 3 + r])
            weights = active.astype(BF16)
            s_tile[hh, slot] = rate
            w_tile[hh, slot] = weights
            attended[q_rows, cols] += dot(weights, act[1, k_rows, cols], NN)

    project(ctx)
    for p in PLANES[2:]:
        take("n%d%d" % (p, 1))
        far_copy(p, 1).start()
        sent.append(lambda p=p: far_copy(p, 1).wait_send())
        due["f%d%d" % (p, 1)] = lambda p=p: far_arrival(p, 1).wait_recv()
    pairs(0, attend)
    for p in PLANES[:2]:
        take("n%d%d" % (p, 1))
    project(right)
    pairs(1, attend)
    for p in PLANES[2:]:
        take("n%d%d" % (p, 0))
    project(left)
    pairs(2, attend)
    for order, p in enumerate(PLANES):
        take("f%d%d" % (p, order // 2))
    project(far)
    pairs(3, attend)

    for step in range(1, 4):
        take("gg%d" % step)

    lane = lax.broadcasted_iota(jnp.int32, (R, 128), 1)

    @pl.loop(0, 4)
    def _(block):
        rows = attended[at(block * R, R), :]
        mean = jnp.mean(rows, axis=1, keepdims=True)
        centered = rows - mean
        flow = gg_all[block].astype(F32) * act[0, at(block * R, R), :].astype(F32)
        packed = jnp.where(lane == 0, mean, 0.0)
        packed = jnp.where(lane == 1, jnp.sum(centered * centered, axis=1, keepdims=True), packed)
        packed = jnp.where(lane == 2, jnp.sum(flow, axis=1, keepdims=True), packed)
        packed = jnp.where(lane == 3, jnp.sum(flow * centered, axis=1, keepdims=True), packed)
        stats_send[block] = packed.T[:8, :]

    def stats_copy(block):
        return copy_to(stats_send, stats_all.at[ctx], st_send.at[block], st_recv.at[ctx], me, block)

    for step in range(1, 4):
        stats_copy((ctx + step) % 4).start()
    stats_all[ctx] = stats_send[...]

    @pl.loop(0, 4)
    def _(piece):
        columns = at(piece * R, R)
        for b in range(4):
            turned[columns, b * R : b * R + R] = normed[b * R : b * R + R, columns].T

    for step in range(1, 4):
        block = (ctx + step) % 4
        sent.append(lambda block=block: stats_copy(block).wait_send())
        copy_to(stats_send, stats_all.at[block], st_send.at[block], st_recv.at[block], me, block).wait_recv()

    for block in range(4):
        parts = [stats_all[c, block] for c in range(4)]
        means = [x[0:1] for x in parts]
        mean = (means[0] + means[1] + means[2] + means[3]) * 0.25
        square = sum(parts[c][1:2] + COLS * (means[c] - mean) * (means[c] - mean) for c in range(4))
        flow = sum(parts[c][2:3] for c in range(4))
        cross = sum(parts[c][3:4] + (means[c] - mean) * parts[c][2:3] for c in range(4))
        inverse = lax.rsqrt(square * (1.0 / D) + EPSILON)
        table = jnp.concatenate(
            (mean, inverse, flow * (1.0 / D), cross * inverse * (1.0 / D), jnp.zeros((124, R), F32)), axis=0
        )
        rows_stat[pl.ds(block * R, R), :] = table.T

    def gated_copy(block):
        return copy_to(gated.at[block], gated_all.at[ctx], gt_send.at[block], gt_recv.at[ctx], me, block)

    @pl.loop(0, 4)
    def _(block):
        rows = at(block * R, R)
        table = rows_stat[rows, :]
        inverse = table[:, 1:2]
        out_unit = (attended[rows, :] - table[:, 0:1]) * inverse
        gate = act[0, rows, :].astype(F32)
        flow = gg_all[block].astype(F32)
        gated[block] = (out_unit * gate).astype(BF16)
        pg[rows, 0:COLS] = (flow * out_unit * slope[0, rows, :]).astype(BF16)
        att_grad[rows, :] = (inverse * (flow * gate - table[:, 2:3] - out_unit * table[:, 3:4])).astype(BF16)

    for step in range(1, 4):
        block = (ctx + step) % 4
        gated_copy(block).start()
        sent.append(lambda block=block: gated_copy(block).wait_send())
        due["gt%d" % step] = lambda block=block: copy_to(gated.at[block], gated_all.at[block], gt_send.at[block], gt_recv.at[block], me, block).wait_recv()
    gated_all[ctx] = gated[ctx]

    def core_copy(which, piece, half):
        cols = pl.ds(half * 512, 512)
        return copy_to(
            g_core.at[which, 1 - core, piece, :, cols], g_core_in.at[which, piece, :, cols], gc_send.at[which, piece, half],
            gc_recv.at[which, piece, half], partner, ctx,
        )

    def along_x(which, other):
        return copy_to(
            ga.at[which, other], ga_in.at[which, x], ga_send.at[which, other], ga_recv.at[which, x],
            (other * 4 + y) * 2 + core, ctx,
        )

    def from_x(which, other):
        return copy_to(
            ga.at[which, other], ga_in.at[which, other], ga_send.at[which, other], ga_recv.at[which, other],
            (other * 4 + y) * 2 + core, ctx,
        )

    def along_y(which, other, piece):
        return copy_to(
            gb.at[which, other, piece], gb_in.at[which, y, piece], gb_send.at[which, other, piece],
            gb_recv.at[which, y, piece], (x * 4 + other) * 2 + core, ctx,
        )

    def from_y(which, other, piece):
        return copy_to(
            gb.at[which, other, piece], gb_in.at[which, other, piece], gb_send.at[which, other, piece],
            gb_recv.at[which, other, piece], (x * 4 + other) * 2 + core, ctx,
        )

    def then_y(which, other):
        return copy_to(
            ha.at[which, other], ha_in.at[which, y], ha_send.at[which, other], ha_recv.at[which, y],
            (x * 4 + other) * 2 + core, ctx,
        )

    def then_from_y(which, other):
        return copy_to(
            ha.at[which, other], ha_in.at[which, other], ha_send.at[which, other], ha_recv.at[which, other],
            (x * 4 + other) * 2 + core, ctx,
        )

    def then_x(which, other):
        return copy_to(
            hb.at[which, other], hb_in.at[which, x], hb_send.at[which, other], hb_recv.at[which, x],
            (other * 4 + y) * 2 + core, ctx,
        )

    def then_from_x(which, other):
        return copy_to(
            hb.at[which, other], hb_in.at[which, other], hb_send.at[which, other], hb_recv.at[which, other],
            (other * 4 + y) * 2 + core, ctx,
        )

    def row_copy(which, block):
        return copy_to(
            g_row.at[which, at(block * 8, 8), :], g_row_in.at[which, ctx], gr_send.at[which, block],
            gr_recv.at[which, ctx], me, block,
        )

    def row_arrival(which, block):
        return copy_to(
            g_row.at[which, at(block * 8, 8), :], g_row_in.at[which, block], gr_send.at[which, block],
            gr_recv.at[which, block], me, block,
        )

    def keep_half(which, piece, half, tile):
        pairs_of = tile.reshape(4, 2, 32, 512)
        cols = slice(half * 512, half * 512 + 512)
        for own in range(2):
            g_core[which, own, piece, :, cols] = pairs_of[:, own].reshape(128, 512).astype(BF16)

    def send_core(which, place, piece, half):
        core_copy(which, piece, half).start()
        sent.append(lambda: core_copy(which, piece, half).wait_send())
        due["gc%d%d%d" % (which, place, half)] = lambda: core_copy(which, piece, half).wait_recv()

    def spread(which, place, piece, half):
        cols = slice(half * 512, half * 512 + 512)
        take("gc%d%d%d" % (which, place, half))
        both = g_core[which, core, piece, :, cols].astype(F32) + g_core_in[which, piece, :, cols].astype(F32)
        both = both.astype(BF16)
        if half == 0:
            ga[which, piece] = both.reshape(4, 32, 512)

            @pl.when(piece != x)
            def _():
                along_x(which, piece).start()

            @pl.when(piece == x)
            def _():
                ga_in[which, x] = ga[which, x]

        else:
            for row in range(4):
                gb[which, row, piece] = both[row * 32 : row * 32 + 32]
            for step in (2, 1, 3):
                other = (y + step) % 4
                along_y(which, other, piece).start()
                sent.append(lambda other=other: along_y(which, other, piece).wait_send())
            gb_in[which, y, piece] = gb[which, y, piece]

    def await_spread(which):
        for step in range(1, 4):
            sent.append(lambda other=(x + step) % 4: along_x(which, other).wait_send())
            due["g0%d%d" % (which, step)] = lambda other=(x + step) % 4: from_x(which, other).wait_recv()

            def wait_rows(other=(y + step) % 4):
                for piece in range(4):
                    from_y(which, other, piece).wait_recv()

            due["g1%d%d" % (which, step)] = wait_rows

    def spread_again(which, half):
        for step in (1, 3, 2):
            take("g%d%d%d" % (half, which, step))
        arrived, held, landed = ((ga_in, ha, ha_in), (gb_in, hb, hb_in))[half]
        total = arrived[which, 0].astype(F32)
        for other in range(1, 4):
            total = total + arrived[which, other].astype(F32)
        held[which] = total.astype(BF16)
        go, come, here = ((then_y, then_from_y, y), (then_x, then_from_x, x))[half]
        for step in (2, 1, 3):
            other = (here + step) % 4
            go(which, other).start()
            sent.append(lambda other=other: go(which, other).wait_send())
            due["h%d%d%d" % (half, which, step)] = lambda other=other: come(which, other).wait_recv()
        landed[which, here] = held[which, here]

    def finish_sum(which):
        for half in range(2):
            for step in (1, 3, 2):
                take("h%d%d%d" % (half, which, step))
            landed = (ha_in, hb_in)[half]
            total = landed[which, 0].astype(F32)
            for other in range(1, 4):
                total = total + landed[which, other].astype(F32)
            g_row[which, :, half * 512 : half * 512 + 512] = total
        for step in (2, 1, 3):
            block = (ctx + step) % 4
            row_copy(which, block).start()
            sent.append(lambda block=block: row_copy(which, block).wait_send())
            due["gr%d%d" % (which, step)] = lambda block=block: row_arrival(which, block).wait_recv()
        g_row_in[which, ctx] = g_row[which, at(ctx * 8, 8), :]

    def attend_back(q, k, r, slot):
        q_rows, k_rows = at(q * R, R), at(k * R, R)
        for hh in range(HEADS):
            cols = slice(hh * DH, hh * DH + DH)
            incoming = att_grad[q_rows, cols]
            change = dot(incoming, act[1, k_rows, cols], NT) * s_tile[hh, slot]
            bias_sum[hh * 3 + r] += change
            rounded = change.astype(BF16)
            dq[q_rows, cols] += dot(rounded, act[3, k_rows, cols], NN)
            dk[k_rows, cols] += dot(rounded, act[2, q_rows, cols], TN)
            dv[k_rows, cols] += dot(w_tile[hh, slot], incoming, TN)

    def close_block(block):
        rows = at(block * R, R)
        pg[rows, 1 * COLS : 1 * COLS + COLS] = (dv[rows, :] * slope[1, rows, :]).astype(BF16)
        pg[rows, 2 * COLS : 2 * COLS + COLS] = (dq[rows, :] * SCALE * slope[2, rows, :]).astype(BF16)
        pg[rows, 3 * COLS : 3 * COLS + COLS] = (dk[rows, :] * SCALE * slope[3, rows, :]).astype(BF16)

    def block_terms(block, half):
        rows = at(block * R, R)
        return dot(pg[rows, :], w_in[half * 512 : half * 512 + 512, :], NT)

    def far_part(side):
        return copy_to(
            ng_far.at[side], ng_far_in.at[side], nf_send.at[side], nf_recv.at[side], me, right if side == 0 else left
        )

    def near_part(side, half, p):
        rows = at((plane + p) % 4 * 64, 64)
        return copy_to(
            ng_near.at[side, half, rows, :], ng_near_in.at[side, half, rows, :], nn_send.at[side, half, p],
            nn_recv.at[side, half, p], me, right if side == 0 else left,
        )

    def send_near(side, half, p):
        near_part(side, half, p).start()
        sent.append(lambda: near_part(side, half, p).wait_send())
        due["nn%d%d%d" % (side, half, p)] = lambda: near_part(side, half, p).wait_recv()

    await_spread(1)
    await_spread(0)
    pairs(3, attend_back)
    close_block(far)
    for side in range(2):
        ng_far[side] = block_terms(far, side).astype(BF16)
        far_part(side).start()
        sent.append(lambda side=side: far_part(side).wait_send())
        due["nf%d" % side] = lambda side=side: far_part(side).wait_recv()

    for place, side in ((2, 1), (1, 0)):
        pairs(place, attend_back)
        block = ordered[place]
        close_block(block)
        ng_near[side, 1 - side] = block_terms(block, 1 - side).astype(BF16)
        for p in PLANES:
            send_near(side, 1 - side, p)
    pairs(0, attend_back)
    close_block(ctx)

    turn = [(x + step) % 4 for step in (2, 1, 3, 0)]
    for step in range(1, 4):
        take("gt%d" % step)
    for place in range(4):
        left_rows = gated_all[turn[place]].T
        for half in range(2):
            keep_half(1, turn[place], half, dot(left_rows, upstream[:, half * 512 : half * 512 + 512], NN))
            send_core(1, place, turn[place], half)
            if place > 1:
                spread(1, place - 2, turn[place - 2], half)

    def input_half(half):
        for place in range(4):
            piece = turn[place]
            keep_half(0, piece, half, dot(turned[at(piece * R, R), :], pg[:, half * 512 : half * 512 + 512], NN))
            send_core(0, place, piece, half)
            if place > 1:
                spread(0, place - 2, turn[place - 2], half)
        return lambda: [spread(0, place, turn[place], half) for place in (2, 3)]

    rest = input_half(0)
    for place in (2, 3):
        for half in range(2):
            spread(1, place, turn[place], half)
    for side in range(2):
        terms = block_terms(right if side == 0 else left, side)
        take("nf%d" % side)
        ng_near[side, side] = (terms + ng_far_in[side].astype(F32)).astype(BF16)
    for p in PLANES:
        for side in range(2):
            send_near(side, side, p)
    rest()
    rest = input_half(1)
    rest()
    spread_again(1, 0)
    spread_again(1, 1)
    for half in range(2):
        ng_own[:, half * 512 : half * 512 + 512] = block_terms(ctx, half)

    sums = jnp.zeros((8, 128), F32)
    tile_row = lax.broadcasted_iota(jnp.int32, (8, 128), 0)
    tile_lane = lax.broadcasted_iota(jnp.int32, (8, 128), 1)
    for hh in range(HEADS):
        for r in range(3):
            reach = (
                lax.broadcasted_iota(jnp.int32, (R, R), 0) - lax.broadcasted_iota(jnp.int32, (R, R), 1) + (r * R + 1)
            )
            low, high = ((0, 8), (1, 9), (8, 9))[r]
            tile = bias_sum[hh * 3 + r]
            for level in range(low, high + 1):
                part = tile
                if level > low:
                    part = jnp.where(reach >= 2**level, part, 0.0)
                if level < high:
                    part = jnp.where(reach < 2 ** (level + 1), part, 0.0)
                total = jnp.sum(jnp.sum(part, axis=0, keepdims=True), axis=1, keepdims=True)
                place = jnp.logical_and(tile_row == ctx * HEADS + hh, tile_lane == level)
                sums = sums + jnp.where(place, total, 0.0)
    b_core[...] = sums
    bias_core = copy_to(b_core, b_core_in, bc_send, bc_recv, partner, ctx)
    bias_core.start()
    sent.append(lambda: bias_core.wait_send())
    due["bc"] = lambda: bias_core.wait_recv()


    def back_copy(dst):
        return copy_to(
            back.at[at(dst * 16, 16), :], back_in.at[at(me * 16, 16), :], r_send.at[dst], r_recv.at[me], dst, ctx
        )

    def back_arrival(src):
        return copy_to(
            back.at[at(src * 16, 16), :], back_in.at[at(src * 16, 16), :], r_send.at[src], r_recv.at[src], src, ctx
        )

    for order, p in enumerate(PLANES):
        if order > 1:
            spread_again(0, order - 2)
        for side in range(2):
            for half in range(2):
                take("nn%d%d%d" % (side, half, p))
        target = (plane + p) % 4
        rows = at(target * 64, 64)
        total = []
        for half in range(2):
            total.append(
                ng_own[rows, half * 512 : half * 512 + 512]
                + ng_near_in[0, half, rows, :].astype(F32)
                + ng_near_in[1, half, rows, :].astype(F32)
            )
        total = jnp.concatenate(total, axis=1)
        values = unit[rows, :]
        plain = jnp.mean(total, axis=1, keepdims=True)
        cross = jnp.mean(total * values, axis=1, keepdims=True)
        change = inverse_in[rows, 0:1] * (total - plain - values * cross)
        result = upstream[rows, :].astype(F32) + change
        back[at(target * 128, 128), :] = split_halves(result).astype(BF16)

        @pl.loop(1 if p == 0 else 0, 8)
        def _(q):
            back_copy(target * 8 + (inner + q) % 8).start()

    back_in[at(me * 16, 16), :] = back[at(me * 16, 16), :]
    sent.append(lambda: ring(32, me, lambda o: back_copy(o).wait_send()))
    due["back"] = lambda: ring(32, me, lambda o: back_arrival(o).wait_recv())

    take("bc")
    b_chip_in[chip] = b_core[...] + b_core_in[...]

    def bias_chip(other):
        return copy_to(
            b_chip_in.at[chip], b_chip_in.at[chip], bk_send.at[other], bk_recv.at[chip], other * 2 + core, ctx
        )

    @pl.loop(1, 16)
    def _(step):
        bias_chip((chip + step) % 16).start()

    sent.append(lambda: ring(16, chip, lambda o: bias_chip(o).wait_send()))
    due["bk"] = lambda: ring(16, chip, lambda other: copy_to(
            b_chip_in.at[other], b_chip_in.at[other], bk_send.at[other], bk_recv.at[other], other * 2 + core, ctx
        ).wait_recv())
    for half in range(2):
        cols = slice(half * 512, half * 512 + 512)
        total = dot(gated_all[0], w_out[0:COLS, cols], NN)
        for c in range(1, 4):
            total = total + dot(gated_all[c], w_out[c * COLS : c * COLS + COLS, cols], NN)
        pairs = balanced[...].astype(F32).reshape(32, 2, 8, 512)
        layer_output[:, cols] = (pairs[:, half].reshape(R, 512) + total).astype(BF16)

    finish_sum(1)
    finish_sum(0)
    take("bk")

    total = b_chip_in[0]
    for other in range(1, 16):
        total = total + b_chip_in[other]
    b_row[...] = total
    b_row_in[ctx] = total
    for step in range(1, 4):
        block = (ctx + step) % 4
        copy_to(b_row, b_row_in.at[ctx], br_send.at[block], br_recv.at[ctx], me, block).start()
        sent.append(lambda block=block: copy_to(b_row, b_row_in.at[ctx], br_send.at[block], br_recv.at[ctx], me, block).wait_send())

    take("back")

    returned = join_halves(back_in[...].astype(F32)).astype(BF16)
    token_gradient[...] = dot(pick[...], returned, NN).astype(BF16)

    for step in range(1, 4):
        block = (ctx + step) % 4
        take("gr0%d" % step)
        take("gr1%d" % step)
        copy_to(b_row, b_row_in.at[block], br_send.at[block], br_recv.at[block], me, block).wait_recv()
    for c in range(4):
        for part in range(4):
            input_gradient[:, part * D + c * COLS : part * D + c * COLS + COLS] = g_row_in[
                0, c, :, part * COLS : part * COLS + COLS
            ]
    output_gradient[...] = g_row_in[1, 0] + g_row_in[1, 1] + g_row_in[1, 2] + g_row_in[1, 3]
    bias_gradient[...] = (b_row_in[0] + b_row_in[1] + b_row_in[2] + b_row_in[3])[:, :NB]

    for fn in sent:
        fn()


def hand_over(*refs):
    for source, target in zip(refs[:5], refs[5:]):
        target[...] = source[...]


def shards(tokens, send_rows, user_lengths, input_weight, output_weight, distance_bias, upstream):
    vmem = pl.BlockSpec(memory_space=pltpu.VMEM)
    smem = pl.BlockSpec(memory_space=pltpu.SMEM)
    hbm = pl.BlockSpec(memory_space=pl.ANY)
    dma = pltpu.SemaphoreType.DMA
    V = pltpu.VMEM
    scratch = [
        V((D, D), BF16), V((D, D), BF16), V((R, R), BF16), V((512, 512), BF16), V((512, 512), BF16),
        V((R, D), F32), V((R, 128), F32), V((LEN, D), BF16), V((4, R, COLS), BF16), V((4, R, COLS), BF16),
        V((4, LEN, COLS), F32), V((4, LEN, COLS), BF16), V((6, R, R), F32),
        V((HEADS, 9, R, R), BF16), V((HEADS, 9, R, R), F32), V((LEN, COLS), F32),
        V((4, 8, R), F32), V((4, 4, 8, R), F32), V((LEN, 128), F32),
        V((4, R, COLS), BF16), V((4, R, COLS), BF16), V((LEN, COLS), BF16),
        V((LEN, COLS), F32), V((LEN, COLS), F32), V((LEN, COLS), F32), V((6, R, R), F32), V((LEN, D), BF16), V((D, LEN), BF16),
        V((LEN, DH), BF16), V((LEN, DH), BF16),
        V((2, R, 512), BF16), V((2, R, 512), BF16), V((2, 2, R, 512), BF16), V((2, 2, R, 512), BF16), V((R, D), F32),
        V((512, 512), BF16), V((512, 512), BF16),
        V((2, 2, 4, 128, D), BF16), V((2, 4, 128, D), BF16),
        V((2, 4, 4, 32, 512), BF16), V((2, 4, 4, 32, 512), BF16), V((2, 4, 4, 32, 512), BF16),
        V((2, 4, 4, 32, 512), BF16), V((2, 4, 32, 512), BF16), V((2, 4, 32, 512), BF16),
        V((2, 4, 32, 512), BF16), V((2, 4, 32, 512), BF16), V((2, 32, D), F32), V((2, 4, 8, D), F32),
        V((8, 128), F32), V((8, 128), F32), V((16, 8, 128), F32), V((8, 128), F32), V((4, 8, 128), F32),
        dma((5,)), dma((32,)), dma((32,)), dma((4,)), dma((4,)), dma((2, 4)), dma((2, 4)), dma((4,)), dma((4,)),
        dma((4,)), dma((4,)), dma((4,)), dma((4,)),
        dma((2,)), dma((2,)), dma((2, 2, 4)), dma((2, 2, 4)), dma((32,)), dma((32,)),
        dma((2, 4, 2)), dma((2, 4, 2)), dma((2, 4)), dma((2, 4)), dma((2, 4, 4)), dma((2, 4, 4)), dma((2, 4)), dma((2, 4)),
        dma((2, 4)), dma((2, 4)), dma((2, 4)), dma((2, 4)),
        dma(()), dma(()), dma((16,)), dma((16,)), dma((4,)), dma((4,)),
    ]
    outs = pl.pallas_call(
        kernel,
        out_shape=(
            jax.ShapeDtypeStruct((R, D), BF16),
            jax.ShapeDtypeStruct((R, D), BF16),
            jax.ShapeDtypeStruct((8, 4 * D), F32),
            jax.ShapeDtypeStruct((8, D), F32),
            jax.ShapeDtypeStruct((8, NB), F32),
        ),
        in_specs=[vmem, vmem, smem, hbm, hbm, smem, vmem],
        out_specs=(vmem,) * 5,
        scratch_shapes=scratch,
        compiler_params=pltpu.CompilerParams(
            collective_id=0, has_side_effects=True, vmem_limit_bytes=60 * 1024 * 1024
        ),
        name="hstu_layer",
    )(tokens, send_rows, user_lengths, input_weight, output_weight, distance_bias, upstream)
    return pl.pallas_call(
        hand_over,
        out_shape=tuple(jax.ShapeDtypeStruct(o.shape, o.dtype) for o in outs),
        in_specs=[vmem] * 5,
        out_specs=(vmem,) * 5,
        name="results",
    )(*outs)


def solution(mesh):
    block = P(("dp", "ctx"), None)
    in_specs = (block, block, P("dp", None), P(), P(), P(), block)
    out_specs = (block, block, block, block, P())
    return jax.shard_map(shards, mesh=mesh, in_specs=in_specs, out_specs=out_specs, check_vma=False)
```

```python
import jax
import jax.numpy as jnp
from jax import lax
from jax.experimental import pallas as pl
from jax.experimental.pallas import tpu as pltpu
from jax.sharding import PartitionSpec as P

PLANES = (0, 1, 3, 2)
AHEAD = 3

H = 8
DH = 128
NB = 12
N_CTX = 4
R = 256
D = 1024
LEN = 1024
COLS = 256
HEADS = 2
EPSILON = 1e-05
HIDDEN = -(2.0**40)
SCALE = DH ** (-0.5)
F32 = jnp.float32
BF16 = jnp.bfloat16
MESH = pl.DeviceIdType.MESH
NN = ((1,), (0,))
NT = ((1,), (1,))
TN = ((0,), (0,))


def dot(left, right, dims):
    return lax.dot_general(left, right, (dims, ((), ())), preferred_element_type=F32)


def at(start, size):
    return pl.ds(pl.multiple_of(start, size), size)


def silu_parts(halved):
    rise = 1.0 + jnp.tanh(halved)
    active = halved * rise
    gate = 0.5 * rise
    return active, gate + active * (1.0 - gate)


def copy_to(src, dst, send_sem, recv_sem, dp, ctx):
    return pltpu.make_async_remote_copy(
        src_ref=src, dst_ref=dst, send_sem=send_sem, recv_sem=recv_sem, device_id=(dp, ctx), device_id_type=MESH
    )


def split_halves(rows):
    count = rows.shape[0] // 8
    left = rows[:, :512].reshape(count, 1, 8, 512)
    right = rows[:, 512:].reshape(count, 1, 8, 512)
    return jnp.concatenate((left, right), axis=1).reshape(count * 16, 512)


def join_halves(pairs):
    count = pairs.shape[0] // 16
    parts = pairs.reshape(count, 2, 8, 512)
    return jnp.concatenate((parts[:, 0].reshape(count * 8, 512), parts[:, 1].reshape(count * 8, 512)), axis=1)


def kernel(
    tokens, send_rows, lengths, weight_in, weight_out, bias_table, upstream,
    layer_output, token_gradient, input_gradient, output_gradient, bias_gradient,
    w_in, w_out, pick, message, balanced, unit, inverse_in, normed, gg_send, gg_all, slope, act, bias_tile,
    w_tile, s_tile, attended, stats_send, stats_all, rows_stat, gated, gated_all, att_grad, dq, dk, dv, bias_sum, pg, turned, q_user, k_user,
    ng_far, ng_far_in, ng_near, ng_near_in, ng_own, back, back_in,
    g_core, g_core_in, ga, ga_in, gb, gb_in, ha, ha_in, hb, hb_in, g_row, g_row_in,
    b_core, b_core_in, b_chip_in, b_row, b_row_in,
    w_sem, a_send, a_recv, gg_ssem, gg_rsem, z_send, z_recv, f_send, f_recv, st_send, st_recv, gt_send, gt_recv,
    nf_send, nf_recv, nn_send, nn_recv, r_send, r_recv, gc_send, gc_recv, ga_send, ga_recv, gb_send, gb_recv, ha_send, ha_recv, hb_send, hb_recv, gr_send, gr_recv,
    bc_send, bc_recv, bk_send, bk_recv, br_send, br_recv,
):
    me = lax.axis_index("dp")
    sent, due = [], {}
    def ring(n, base, fn):
        @pl.loop(1, n)
        def _(step):
            fn((base + step) % n)
    def take(key):
        due.pop(key)()
    ctx = lax.axis_index("ctx")
    plane, inner = me // 8, me % 8
    chip, core = me // 2, me % 2
    partner = chip * 2 + (1 - core)
    right, left, far = (ctx + 1) % 4, (ctx + 3) % 4, (ctx + 2) % 4
    x, y = chip // 4, chip % 4
    ordered = (ctx, right, left, far)

    barrier = pltpu.get_barrier_semaphore()

    @pl.loop(1, 32)
    def _(step):
        pl.semaphore_signal(barrier, inc=1, device_id=((me + step) % 32, ctx), device_id_type=MESH)

    for step in range(1, 4):
        pl.semaphore_signal(barrier, inc=1, device_id=(me, (ctx + step) % 4), device_id_type=MESH)

    out_copy = pltpu.make_async_copy(weight_out, w_out, w_sem.at[4])
    out_copy.start()
    in_copies = []
    for part in range(4):
        columns = pl.ds(pl.multiple_of(part * D + ctx * COLS, COLS), COLS)
        in_copies.append(pltpu.make_async_copy(weight_in.at[:, columns], w_in.at[:, pl.ds(part * COLS, COLS)], w_sem.at[part]))
        in_copies[-1].start()
    due["w4"] = out_copy.wait
    for part in range(4):
        due["w%d" % part] = in_copies[part].wait

    rows_of = lax.broadcasted_iota(jnp.int32, (R, R), 0)
    pick[...] = jnp.where(rows_of == send_rows[...], 1.0, 0.0).astype(BF16)
    message[...] = split_halves(dot(pick[...], tokens[...], TN)).astype(BF16)

    take("w4")

    def gg_copy(block):
        return copy_to(
            gg_send.at[block], gg_all.at[ctx], gg_ssem.at[block], gg_rsem.at[ctx], me, block
        )

    for block in range(4):
        gg_send[block] = dot(upstream[...], w_out[block * COLS : block * COLS + COLS, :], NT).astype(BF16)

    pl.semaphore_wait(barrier, 34)

    def token_copy(dst):
        return copy_to(
            message.at[at(dst * 16, 16), :], balanced.at[at(me * 16, 16), :], a_send.at[dst], a_recv.at[me], dst, ctx
        )

    def token_arrival(src):
        return copy_to(
            message.at[at(src * 16, 16), :], balanced.at[at(src * 16, 16), :], a_send.at[src], a_recv.at[src], src, ctx
        )

    def send_plane(p):
        @pl.loop(1 if p == 0 else 0, 8)
        def _(q):
            token_copy((plane + p) % 4 * 8 + (inner + q) % 8).start()

    for p in PLANES[:AHEAD]:
        send_plane(p)
    balanced[at(me * 16, 16), :] = message[at(me * 16, 16), :]
    sent.append(lambda: ring(32, me, lambda o: token_copy(o).wait_send()))

    for step in (2, 1, 3):
        block = (ctx + step) % 4
        gg_copy(block).start()
        sent.append(lambda block=block: gg_copy(block).wait_send())
        due["gg%d" % step] = lambda block=block: copy_to(
            gg_send.at[block], gg_all.at[block], gg_ssem.at[block], gg_rsem.at[block], me, block
        ).wait_recv()
    gg_all[ctx] = gg_send[ctx]

    def near_copy(p, side):
        rows = at(ctx * R + (plane + 4 - p) % 4 * 64, 64)
        return copy_to(
            normed.at[rows, :], normed.at[rows, :], z_send.at[side, p], z_recv.at[side, p], me, right if side == 0 else left
        )

    def near_arrival(p, side):
        rows = at((left if side == 0 else right) * R + (plane + 4 - p) % 4 * 64, 64)
        return copy_to(
            normed.at[rows, :], normed.at[rows, :], z_send.at[side, p], z_recv.at[side, p], me, right if side == 0 else left
        )

    def far_copy(p, side):
        rows = at((left if side == 0 else right) * R + (plane + 4 - p) % 4 * 64, 64)
        return copy_to(
            normed.at[rows, :], normed.at[rows, :], f_send.at[p], f_recv.at[p], me, right if side == 0 else left
        )

    def far_arrival(p, side):
        rows = at(far * R + (plane + 4 - p) % 4 * 64, 64)
        return copy_to(
            normed.at[rows, :], normed.at[rows, :], f_send.at[p], f_recv.at[p], me, right if side == 0 else left
        )

    for order, p in enumerate(PLANES):
        source = (plane + 4 - p) % 4

        @pl.loop(1 if p == 0 else 0, 8)
        def _(q):
            token_arrival(source * 8 + (inner + 8 - q) % 8).wait_recv()

        if order + AHEAD < 4:
            send_plane(PLANES[order + AHEAD])
        rows = join_halves(balanced[at(source * 128, 128), :].astype(F32))
        mean = jnp.mean(rows, axis=1, keepdims=True)
        centered = rows - mean
        inverse = lax.rsqrt(jnp.mean(centered * centered, axis=1, keepdims=True) + EPSILON)
        values = centered * inverse
        unit[at(source * 64, 64), :] = values
        inverse_in[at(source * 64, 64), :] = jnp.broadcast_to(inverse, (64, 128))
        normed[at(ctx * R + source * 64, 64), :] = values.astype(BF16)
        for side in range(2):
            near_copy(p, side).start()
            sent.append(lambda p=p, side=side: near_copy(p, side).wait_send())
            due["n%d%d" % (p, side)] = lambda p=p, side=side: near_arrival(p, side).wait_recv()

    for part in range(4):
        take("w%d" % part)

    attended[...] = jnp.zeros((LEN, COLS), F32)
    dq[...] = jnp.zeros((LEN, COLS), F32)
    dk[...] = jnp.zeros((LEN, COLS), F32)
    dv[...] = jnp.zeros((LEN, COLS), F32)
    bias_sum[...] = jnp.zeros((6, R, R), F32)

    end_0 = lengths[0, 0]
    end_1 = end_0 + lengths[0, 1]
    position = lax.broadcasted_iota(jnp.int32, (LEN, DH), 0)
    user = jnp.where(position >= end_0, 1, 0) + jnp.where(position >= end_1, 1, 0)
    same = user == lax.broadcasted_iota(jnp.int32, (LEN, DH), 1)
    q_user[...] = jnp.where(same, 1.0, 0.0).astype(BF16)
    k_user[...] = jnp.where(same, 0.0, HIDDEN).astype(BF16)

    def project(block):
        rows = at(block * R, R)
        for half in range(2):
            active, rate = silu_parts(0.5 * dot(normed[rows, :], w_in[:, half * 512 : half * 512 + 512], NN))
            for part in range(2):
                cols = slice(part * COLS, part * COLS + COLS)
                act[half * 2 + part, rows, :] = active[:, cols].astype(BF16)
                slope[half * 2 + part, rows, :] = rate[:, cols]

    for p in PLANES[:2]:
        take("n%d%d" % (p, 0))
        far_copy(p, 0).start()
        sent.append(lambda p=p: far_copy(p, 0).wait_send())
        due["f%d%d" % (p, 0)] = lambda p=p: far_arrival(p, 0).wait_recv()

    for hh in range(HEADS):
        for r in range(3):
            reach = (
                lax.broadcasted_iota(jnp.int32, (R, R), 0) - lax.broadcasted_iota(jnp.int32, (R, R), 1) + (r * R + 1)
            )
            low, high = ((0, 8), (1, 9), (8, 9))[r]
            tile = jnp.full((R, R), 0.5 * bias_table[ctx * HEADS + hh, low], F32)
            for level in range(low + 1, high + 1):
                tile = jnp.where(reach >= 2**level, 0.5 * bias_table[ctx * HEADS + hh, level], tile)
            if r == 0:
                tile = jnp.where(reach >= 1, tile, HIDDEN)
            bias_tile[hh * 3 + r] = tile

    def pairs(place, body):
        @pl.loop(0, place + 1)
        def _(other):
            a = ordered[place]
            b = (ctx + other + other // 2 - 2 * (other // 3)) % 4
            a_last = (a - b + 4) // 4
            q = b + (a - b) * a_last
            k = a + b - q
            r = q - k

            @pl.when(r < 3)
            def _():
                body(q, k, r, q + 3 * r - r // 2)

    def attend(q, k, r, slot):
        q_rows, k_rows = at(q * R, R), at(k * R, R)
        for hh in range(HEADS):
            cols = slice(hh * DH, hh * DH + DH)
            query = jnp.concatenate((act[2, q_rows, cols], q_user[q_rows, :]), axis=1)
            keys = jnp.concatenate((act[3, k_rows, cols], k_user[k_rows, :]), axis=1)
            active, rate = silu_parts(dot(query, keys, NT) * (0.5 * SCALE) + bias_tile[hh * 3 + r])
            weights = active.astype(BF16)
            s_tile[hh, slot] = rate
            w_tile[hh, slot] = weights
            attended[q_rows, cols] += dot(weights, act[1, k_rows, cols], NN)

    project(ctx)
    for p in PLANES[2:]:
        take("n%d%d" % (p, 1))
        far_copy(p, 1).start()
        sent.append(lambda p=p: far_copy(p, 1).wait_send())
        due["f%d%d" % (p, 1)] = lambda p=p: far_arrival(p, 1).wait_recv()
    pairs(0, attend)
    for p in PLANES[:2]:
        take("n%d%d" % (p, 1))
    project(right)
    pairs(1, attend)
    for p in PLANES[2:]:
        take("n%d%d" % (p, 0))
    project(left)
    pairs(2, attend)
    for order, p in enumerate(PLANES):
        take("f%d%d" % (p, order // 2))
    project(far)
    pairs(3, attend)

    for step in range(1, 4):
        take("gg%d" % step)

    lane = lax.broadcasted_iota(jnp.int32, (R, 128), 1)

    @pl.loop(0, 4)
    def _(block):
        rows = attended[at(block * R, R), :]
        mean = jnp.mean(rows, axis=1, keepdims=True)
        centered = rows - mean
        flow = gg_all[block].astype(F32) * act[0, at(block * R, R), :].astype(F32)
        packed = jnp.where(lane == 0, mean, 0.0)
        packed = jnp.where(lane == 1, jnp.sum(centered * centered, axis=1, keepdims=True), packed)
        packed = jnp.where(lane == 2, jnp.sum(flow, axis=1, keepdims=True), packed)
        packed = jnp.where(lane == 3, jnp.sum(flow * centered, axis=1, keepdims=True), packed)
        stats_send[block] = packed.T[:8, :]

    def stats_copy(block):
        return copy_to(stats_send, stats_all.at[ctx], st_send.at[block], st_recv.at[ctx], me, block)

    for step in range(1, 4):
        stats_copy((ctx + step) % 4).start()
    stats_all[ctx] = stats_send[...]

    @pl.loop(0, 4)
    def _(piece):
        columns = at(piece * R, R)
        for b in range(4):
            turned[columns, b * R : b * R + R] = normed[b * R : b * R + R, columns].T

    for step in range(1, 4):
        block = (ctx + step) % 4
        sent.append(lambda block=block: stats_copy(block).wait_send())
        copy_to(stats_send, stats_all.at[block], st_send.at[block], st_recv.at[block], me, block).wait_recv()

    for block in range(4):
        parts = [stats_all[c, block] for c in range(4)]
        means = [x[0:1] for x in parts]
        mean = (means[0] + means[1] + means[2] + means[3]) * 0.25
        square = sum(parts[c][1:2] + COLS * (means[c] - mean) * (means[c] - mean) for c in range(4))
        flow = sum(parts[c][2:3] for c in range(4))
        cross = sum(parts[c][3:4] + (means[c] - mean) * parts[c][2:3] for c in range(4))
        inverse = lax.rsqrt(square * (1.0 / D) + EPSILON)
        table = jnp.concatenate(
            (mean, inverse, flow * (1.0 / D), cross * inverse * (1.0 / D), jnp.zeros((124, R), F32)), axis=0
        )
        rows_stat[pl.ds(block * R, R), :] = table.T

    def gated_copy(block):
        return copy_to(gated.at[block], gated_all.at[ctx], gt_send.at[block], gt_recv.at[ctx], me, block)

    @pl.loop(0, 4)
    def _(block):
        rows = at(block * R, R)
        table = rows_stat[rows, :]
        inverse = table[:, 1:2]
        out_unit = (attended[rows, :] - table[:, 0:1]) * inverse
        gate = act[0, rows, :].astype(F32)
        flow = gg_all[block].astype(F32)
        gated[block] = (out_unit * gate).astype(BF16)
        pg[rows, 0:COLS] = (flow * out_unit * slope[0, rows, :]).astype(BF16)
        att_grad[rows, :] = (inverse * (flow * gate - table[:, 2:3] - out_unit * table[:, 3:4])).astype(BF16)

    for step in range(1, 4):
        block = (ctx + step) % 4
        gated_copy(block).start()
        sent.append(lambda block=block: gated_copy(block).wait_send())
        due["gt%d" % step] = lambda block=block: copy_to(gated.at[block], gated_all.at[block], gt_send.at[block], gt_recv.at[block], me, block).wait_recv()
    gated_all[ctx] = gated[ctx]

    def core_copy(which, piece, half):
        cols = pl.ds(half * 512, 512)
        return copy_to(
            g_core.at[which, 1 - core, piece, :, cols], g_core_in.at[which, piece, :, cols], gc_send.at[which, piece, half],
            gc_recv.at[which, piece, half], partner, ctx,
        )

    def along_x(which, other):
        return copy_to(
            ga.at[which, other], ga_in.at[which, x], ga_send.at[which, other], ga_recv.at[which, x],
            (other * 4 + y) * 2 + core, ctx,
        )

    def from_x(which, other):
        return copy_to(
            ga.at[which, other], ga_in.at[which, other], ga_send.at[which, other], ga_recv.at[which, other],
            (other * 4 + y) * 2 + core, ctx,
        )

    def along_y(which, other, piece):
        return copy_to(
            gb.at[which, other, piece], gb_in.at[which, y, piece], gb_send.at[which, other, piece],
            gb_recv.at[which, y, piece], (x * 4 + other) * 2 + core, ctx,
        )

    def from_y(which, other, piece):
        return copy_to(
            gb.at[which, other, piece], gb_in.at[which, other, piece], gb_send.at[which, other, piece],
            gb_recv.at[which, other, piece], (x * 4 + other) * 2 + core, ctx,
        )

    def then_y(which, other):
        return copy_to(
            ha.at[which, other], ha_in.at[which, y], ha_send.at[which, other], ha_recv.at[which, y],
            (x * 4 + other) * 2 + core, ctx,
        )

    def then_from_y(which, other):
        return copy_to(
            ha.at[which, other], ha_in.at[which, other], ha_send.at[which, other], ha_recv.at[which, other],
            (x * 4 + other) * 2 + core, ctx,
        )

    def then_x(which, other):
        return copy_to(
            hb.at[which, other], hb_in.at[which, x], hb_send.at[which, other], hb_recv.at[which, x],
            (other * 4 + y) * 2 + core, ctx,
        )

    def then_from_x(which, other):
        return copy_to(
            hb.at[which, other], hb_in.at[which, other], hb_send.at[which, other], hb_recv.at[which, other],
            (other * 4 + y) * 2 + core, ctx,
        )

    def row_copy(which, block):
        return copy_to(
            g_row.at[which, at(block * 8, 8), :], g_row_in.at[which, ctx], gr_send.at[which, block],
            gr_recv.at[which, ctx], me, block,
        )

    def row_arrival(which, block):
        return copy_to(
            g_row.at[which, at(block * 8, 8), :], g_row_in.at[which, block], gr_send.at[which, block],
            gr_recv.at[which, block], me, block,
        )

    def keep_half(which, piece, half, tile):
        pairs_of = tile.reshape(4, 2, 32, 512)
        cols = slice(half * 512, half * 512 + 512)
        for own in range(2):
            g_core[which, own, piece, :, cols] = pairs_of[:, own].reshape(128, 512).astype(BF16)

    def send_core(which, place, piece, half):
        core_copy(which, piece, half).start()
        sent.append(lambda: core_copy(which, piece, half).wait_send())
        due["gc%d%d%d" % (which, place, half)] = lambda: core_copy(which, piece, half).wait_recv()

    def spread(which, place, piece, half):
        cols = slice(half * 512, half * 512 + 512)
        take("gc%d%d%d" % (which, place, half))
        both = g_core[which, core, piece, :, cols].astype(F32) + g_core_in[which, piece, :, cols].astype(F32)
        both = both.astype(BF16)
        if half == 0:
            ga[which, piece] = both.reshape(4, 32, 512)

            @pl.when(piece != x)
            def _():
                along_x(which, piece).start()

            @pl.when(piece == x)
            def _():
                ga_in[which, x] = ga[which, x]

        else:
            for row in range(4):
                gb[which, row, piece] = both[row * 32 : row * 32 + 32]
            for step in (2, 1, 3):
                other = (y + step) % 4
                along_y(which, other, piece).start()
                sent.append(lambda other=other: along_y(which, other, piece).wait_send())
            gb_in[which, y, piece] = gb[which, y, piece]

    def await_spread(which):
        for step in range(1, 4):
            sent.append(lambda other=(x + step) % 4: along_x(which, other).wait_send())
            due["g0%d%d" % (which, step)] = lambda other=(x + step) % 4: from_x(which, other).wait_recv()

            def wait_rows(other=(y + step) % 4):
                for piece in range(4):
                    from_y(which, other, piece).wait_recv()

            due["g1%d%d" % (which, step)] = wait_rows

    def spread_again(which, half):
        for step in (1, 3, 2):
            take("g%d%d%d" % (half, which, step))
        arrived, held, landed = ((ga_in, ha, ha_in), (gb_in, hb, hb_in))[half]
        total = arrived[which, 0].astype(F32)
        for other in range(1, 4):
            total = total + arrived[which, other].astype(F32)
        held[which] = total.astype(BF16)
        go, come, here = ((then_y, then_from_y, y), (then_x, then_from_x, x))[half]
        for step in (2, 1, 3):
            other = (here + step) % 4
            go(which, other).start()
            sent.append(lambda other=other: go(which, other).wait_send())
            due["h%d%d%d" % (half, which, step)] = lambda other=other: come(which, other).wait_recv()
        landed[which, here] = held[which, here]

    def finish_sum(which):
        for half in range(2):
            for step in (1, 3, 2):
                take("h%d%d%d" % (half, which, step))
            landed = (ha_in, hb_in)[half]
            total = landed[which, 0].astype(F32)
            for other in range(1, 4):
                total = total + landed[which, other].astype(F32)
            g_row[which, :, half * 512 : half * 512 + 512] = total
        for step in (2, 1, 3):
            block = (ctx + step) % 4
            row_copy(which, block).start()
            sent.append(lambda block=block: row_copy(which, block).wait_send())
            due["gr%d%d" % (which, step)] = lambda block=block: row_arrival(which, block).wait_recv()
        g_row_in[which, ctx] = g_row[which, at(ctx * 8, 8), :]

    def attend_back(q, k, r, slot):
        q_rows, k_rows = at(q * R, R), at(k * R, R)
        for hh in range(HEADS):
            cols = slice(hh * DH, hh * DH + DH)
            incoming = att_grad[q_rows, cols]
            change = dot(incoming, act[1, k_rows, cols], NT) * s_tile[hh, slot]
            bias_sum[hh * 3 + r] += change
            rounded = change.astype(BF16)
            dq[q_rows, cols] += dot(rounded, act[3, k_rows, cols], NN)
            dk[k_rows, cols] += dot(rounded, act[2, q_rows, cols], TN)
            dv[k_rows, cols] += dot(w_tile[hh, slot], incoming, TN)

    def close_block(block):
        rows = at(block * R, R)
        pg[rows, 1 * COLS : 1 * COLS + COLS] = (dv[rows, :] * slope[1, rows, :]).astype(BF16)
        pg[rows, 2 * COLS : 2 * COLS + COLS] = (dq[rows, :] * SCALE * slope[2, rows, :]).astype(BF16)
        pg[rows, 3 * COLS : 3 * COLS + COLS] = (dk[rows, :] * SCALE * slope[3, rows, :]).astype(BF16)

    def block_terms(block, half):
        rows = at(block * R, R)
        return dot(pg[rows, :], w_in[half * 512 : half * 512 + 512, :], NT)

    def far_part(side):
        return copy_to(
            ng_far.at[side], ng_far_in.at[side], nf_send.at[side], nf_recv.at[side], me, right if side == 0 else left
        )

    def near_part(side, half, p):
        rows = at((plane + p) % 4 * 64, 64)
        return copy_to(
            ng_near.at[side, half, rows, :], ng_near_in.at[side, half, rows, :], nn_send.at[side, half, p],
            nn_recv.at[side, half, p], me, right if side == 0 else left,
        )

    def send_near(side, half, p):
        near_part(side, half, p).start()
        sent.append(lambda: near_part(side, half, p).wait_send())
        due["nn%d%d%d" % (side, half, p)] = lambda: near_part(side, half, p).wait_recv()

    await_spread(1)
    await_spread(0)
    pairs(3, attend_back)
    close_block(far)
    for side in range(2):
        ng_far[side] = block_terms(far, side).astype(BF16)
        far_part(side).start()
        sent.append(lambda side=side: far_part(side).wait_send())
        due["nf%d" % side] = lambda side=side: far_part(side).wait_recv()

    for place, side in ((2, 1), (1, 0)):
        pairs(place, attend_back)
        block = ordered[place]
        close_block(block)
        ng_near[side, 1 - side] = block_terms(block, 1 - side).astype(BF16)
        for p in PLANES:
            send_near(side, 1 - side, p)
    pairs(0, attend_back)
    close_block(ctx)

    turn = [(x + step) % 4 for step in (2, 1, 3, 0)]
    for step in range(1, 4):
        take("gt%d" % step)
    for place in range(4):
        left_rows = gated_all[turn[place]].T
        for half in range(2):
            keep_half(1, turn[place], half, dot(left_rows, upstream[:, half * 512 : half * 512 + 512], NN))
            send_core(1, place, turn[place], half)
            if place > 1:
                spread(1, place - 2, turn[place - 2], half)

    def input_half(half):
        for place in range(4):
            piece = turn[place]
            keep_half(0, piece, half, dot(turned[at(piece * R, R), :], pg[:, half * 512 : half * 512 + 512], NN))
            send_core(0, place, piece, half)
            if place > 1:
                spread(0, place - 2, turn[place - 2], half)
        return lambda: [spread(0, place, turn[place], half) for place in (2, 3)]

    rest = input_half(0)
    for place in (2, 3):
        for half in range(2):
            spread(1, place, turn[place], half)
    for side in range(2):
        terms = block_terms(right if side == 0 else left, side)
        take("nf%d" % side)
        ng_near[side, side] = (terms + ng_far_in[side].astype(F32)).astype(BF16)
    for p in PLANES:
        for side in range(2):
            send_near(side, side, p)
    rest()
    rest = input_half(1)
    rest()
    spread_again(1, 0)
    spread_again(1, 1)
    for half in range(2):
        ng_own[:, half * 512 : half * 512 + 512] = block_terms(ctx, half)

    sums = jnp.zeros((8, 128), F32)
    tile_row = lax.broadcasted_iota(jnp.int32, (8, 128), 0)
    tile_lane = lax.broadcasted_iota(jnp.int32, (8, 128), 1)
    for hh in range(HEADS):
        for r in range(3):
            reach = (
                lax.broadcasted_iota(jnp.int32, (R, R), 0) - lax.broadcasted_iota(jnp.int32, (R, R), 1) + (r * R + 1)
            )
            low, high = ((0, 8), (1, 9), (8, 9))[r]
            tile = bias_sum[hh * 3 + r]
            for level in range(low, high + 1):
                part = tile
                if level > low:
                    part = jnp.where(reach >= 2**level, part, 0.0)
                if level < high:
                    part = jnp.where(reach < 2 ** (level + 1), part, 0.0)
                total = jnp.sum(jnp.sum(part, axis=0, keepdims=True), axis=1, keepdims=True)
                place = jnp.logical_and(tile_row == ctx * HEADS + hh, tile_lane == level)
                sums = sums + jnp.where(place, total, 0.0)
    b_core[...] = sums
    bias_core = copy_to(b_core, b_core_in, bc_send, bc_recv, partner, ctx)
    bias_core.start()
    sent.append(lambda: bias_core.wait_send())
    due["bc"] = lambda: bias_core.wait_recv()


    def back_copy(dst):
        return copy_to(
            back.at[at(dst * 16, 16), :], back_in.at[at(me * 16, 16), :], r_send.at[dst], r_recv.at[me], dst, ctx
        )

    def back_arrival(src):
        return copy_to(
            back.at[at(src * 16, 16), :], back_in.at[at(src * 16, 16), :], r_send.at[src], r_recv.at[src], src, ctx
        )

    for order, p in enumerate(PLANES):
        if order < 2:
            spread_again(0, order)
        for side in range(2):
            for half in range(2):
                take("nn%d%d%d" % (side, half, p))
        target = (plane + p) % 4
        rows = at(target * 64, 64)
        total = []
        for half in range(2):
            total.append(
                ng_own[rows, half * 512 : half * 512 + 512]
                + ng_near_in[0, half, rows, :].astype(F32)
                + ng_near_in[1, half, rows, :].astype(F32)
            )
        total = jnp.concatenate(total, axis=1)
        values = unit[rows, :]
        plain = jnp.mean(total, axis=1, keepdims=True)
        cross = jnp.mean(total * values, axis=1, keepdims=True)
        change = inverse_in[rows, 0:1] * (total - plain - values * cross)
        result = upstream[rows, :].astype(F32) + change
        back[at(target * 128, 128), :] = split_halves(result).astype(BF16)

        @pl.loop(1 if p == 0 else 0, 8)
        def _(q):
            back_copy(target * 8 + (inner + q) % 8).start()

    back_in[at(me * 16, 16), :] = back[at(me * 16, 16), :]
    sent.append(lambda: ring(32, me, lambda o: back_copy(o).wait_send()))
    due["back"] = lambda: ring(32, me, lambda o: back_arrival(o).wait_recv())

    take("bc")
    b_chip_in[chip] = b_core[...] + b_core_in[...]

    def bias_chip(other):
        return copy_to(
            b_chip_in.at[chip], b_chip_in.at[chip], bk_send.at[other], bk_recv.at[chip], other * 2 + core, ctx
        )

    @pl.loop(1, 16)
    def _(step):
        bias_chip((chip + step) % 16).start()

    sent.append(lambda: ring(16, chip, lambda o: bias_chip(o).wait_send()))
    due["bk"] = lambda: ring(16, chip, lambda other: copy_to(
            b_chip_in.at[other], b_chip_in.at[other], bk_send.at[other], bk_recv.at[other], other * 2 + core, ctx
        ).wait_recv())
    for half in range(2):
        cols = slice(half * 512, half * 512 + 512)
        total = dot(gated_all[0], w_out[0:COLS, cols], NN)
        for c in range(1, 4):
            total = total + dot(gated_all[c], w_out[c * COLS : c * COLS + COLS, cols], NN)
        pairs = balanced[...].astype(F32).reshape(32, 2, 8, 512)
        layer_output[:, cols] = (pairs[:, half].reshape(R, 512) + total).astype(BF16)

    finish_sum(1)
    finish_sum(0)
    take("bk")

    total = b_chip_in[0]
    for other in range(1, 16):
        total = total + b_chip_in[other]
    b_row[...] = total
    b_row_in[ctx] = total
    for step in range(1, 4):
        block = (ctx + step) % 4
        copy_to(b_row, b_row_in.at[ctx], br_send.at[block], br_recv.at[ctx], me, block).start()
        sent.append(lambda block=block: copy_to(b_row, b_row_in.at[ctx], br_send.at[block], br_recv.at[ctx], me, block).wait_send())

    take("back")

    returned = join_halves(back_in[...].astype(F32)).astype(BF16)
    token_gradient[...] = dot(pick[...], returned, NN).astype(BF16)

    for step in range(1, 4):
        block = (ctx + step) % 4
        take("gr0%d" % step)
        take("gr1%d" % step)
        copy_to(b_row, b_row_in.at[block], br_send.at[block], br_recv.at[block], me, block).wait_recv()
    for c in range(4):
        for part in range(4):
            input_gradient[:, part * D + c * COLS : part * D + c * COLS + COLS] = g_row_in[
                0, c, :, part * COLS : part * COLS + COLS
            ]
    output_gradient[...] = g_row_in[1, 0] + g_row_in[1, 1] + g_row_in[1, 2] + g_row_in[1, 3]
    bias_gradient[...] = (b_row_in[0] + b_row_in[1] + b_row_in[2] + b_row_in[3])[:, :NB]

    for fn in sent:
        fn()


def hand_over(*refs):
    for source, target in zip(refs[:5], refs[5:]):
        target[...] = source[...]


def shards(tokens, send_rows, user_lengths, input_weight, output_weight, distance_bias, upstream):
    vmem = pl.BlockSpec(memory_space=pltpu.VMEM)
    smem = pl.BlockSpec(memory_space=pltpu.SMEM)
    hbm = pl.BlockSpec(memory_space=pl.ANY)
    dma = pltpu.SemaphoreType.DMA
    V = pltpu.VMEM
    scratch = [
        V((D, D), BF16), V((D, D), BF16), V((R, R), BF16), V((512, 512), BF16), V((512, 512), BF16),
        V((R, D), F32), V((R, 128), F32), V((LEN, D), BF16), V((4, R, COLS), BF16), V((4, R, COLS), BF16),
        V((4, LEN, COLS), F32), V((4, LEN, COLS), BF16), V((6, R, R), F32),
        V((HEADS, 9, R, R), BF16), V((HEADS, 9, R, R), F32), V((LEN, COLS), F32),
        V((4, 8, R), F32), V((4, 4, 8, R), F32), V((LEN, 128), F32),
        V((4, R, COLS), BF16), V((4, R, COLS), BF16), V((LEN, COLS), BF16),
        V((LEN, COLS), F32), V((LEN, COLS), F32), V((LEN, COLS), F32), V((6, R, R), F32), V((LEN, D), BF16), V((D, LEN), BF16),
        V((LEN, DH), BF16), V((LEN, DH), BF16),
        V((2, R, 512), BF16), V((2, R, 512), BF16), V((2, 2, R, 512), BF16), V((2, 2, R, 512), BF16), V((R, D), F32),
        V((512, 512), BF16), V((512, 512), BF16),
        V((2, 2, 4, 128, D), BF16), V((2, 4, 128, D), BF16),
        V((2, 4, 4, 32, 512), BF16), V((2, 4, 4, 32, 512), BF16), V((2, 4, 4, 32, 512), BF16),
        V((2, 4, 4, 32, 512), BF16), V((2, 4, 32, 512), BF16), V((2, 4, 32, 512), BF16),
        V((2, 4, 32, 512), BF16), V((2, 4, 32, 512), BF16), V((2, 32, D), F32), V((2, 4, 8, D), F32),
        V((8, 128), F32), V((8, 128), F32), V((16, 8, 128), F32), V((8, 128), F32), V((4, 8, 128), F32),
        dma((5,)), dma((32,)), dma((32,)), dma((4,)), dma((4,)), dma((2, 4)), dma((2, 4)), dma((4,)), dma((4,)),
        dma((4,)), dma((4,)), dma((4,)), dma((4,)),
        dma((2,)), dma((2,)), dma((2, 2, 4)), dma((2, 2, 4)), dma((32,)), dma((32,)),
        dma((2, 4, 2)), dma((2, 4, 2)), dma((2, 4)), dma((2, 4)), dma((2, 4, 4)), dma((2, 4, 4)), dma((2, 4)), dma((2, 4)),
        dma((2, 4)), dma((2, 4)), dma((2, 4)), dma((2, 4)),
        dma(()), dma(()), dma((16,)), dma((16,)), dma((4,)), dma((4,)),
    ]
    outs = pl.pallas_call(
        kernel,
        out_shape=(
            jax.ShapeDtypeStruct((R, D), BF16),
            jax.ShapeDtypeStruct((R, D), BF16),
            jax.ShapeDtypeStruct((8, 4 * D), F32),
            jax.ShapeDtypeStruct((8, D), F32),
            jax.ShapeDtypeStruct((8, NB), F32),
        ),
        in_specs=[vmem, vmem, smem, hbm, hbm, smem, vmem],
        out_specs=(vmem,) * 5,
        scratch_shapes=scratch,
        compiler_params=pltpu.CompilerParams(
            collective_id=0, has_side_effects=True, vmem_limit_bytes=60 * 1024 * 1024
        ),
        name="hstu_layer",
    )(tokens, send_rows, user_lengths, input_weight, output_weight, distance_bias, upstream)
    return pl.pallas_call(
        hand_over,
        out_shape=tuple(jax.ShapeDtypeStruct(o.shape, o.dtype) for o in outs),
        in_specs=[vmem] * 5,
        out_specs=(vmem,) * 5,
        name="results",
    )(*outs)


def solution(mesh):
    block = P(("dp", "ctx"), None)
    in_specs = (block, block, P("dp", None), P(), P(), P(), block)
    out_specs = (block, block, block, block, P())
    return jax.shard_map(shards, mesh=mesh, in_specs=in_specs, out_specs=out_specs, check_vma=False)
```
